256 devices in a mesh: dp: 8 (over z_lo, x), seq: 32 (over z_hi, y, core).
Axes of the slice: x: 4, y: 4, z: 8 (z_hi: 4, z_lo: 2; z = z_hi * 2 + z_lo), core: 2. Of those that a mesh axis runs over, the one named last changes fastest.
Arguments:
- query: bfloat16 [8, 4096, 2048], P('dp', 'seq'), may hold values from -5 to 5
- keys: bfloat16 [8, 4096, 1024], P('dp', 'seq'), may hold values from -5 to 5
- values: bfloat16 [8, 4096, 1024], P('dp', 'seq'), may hold values from -6 to 6
- out_weight: bfloat16 [2048, 1920], P('dp'), may hold values from -0.125 to 0.125
- out_grad: bfloat16 [8, 4096, 1920], P('dp', 'seq'), may hold values from -6 to 6
- doc_blocks: int32 [8, 8], P('dp'), may hold values from 1 to 8, 32 in all within a row
Outputs:
- layer_out: bfloat16 [8, 4096, 1920], P('dp', 'seq')
- query_grad: bfloat16 [8, 4096, 2048], P('dp', 'seq')
- key_gradient: bfloat16 [8, 4096, 1024], P('dp', 'seq')
- value_gradient: bfloat16 [8, 4096, 1024], P('dp', 'seq')
- weight_grad: float32 [2048, 1920], P(('dp', 'seq'))
The draws below stay inside these ranges and needn't reach their ends.
Inputs may be any that keep to these rules, and one draw needn't show every extreme that they name: `doc_blocks`: each row holds the lengths, in blocks of 128 tokens, of 8 documents that fill the sequence's 32 blocks; the longest has exactly 8 blocks.
All inputs are finite; a program needn't handle non-finite values.
Results may differ from the reference program's by a relative error of at most 0.02.
Values may be sent and summed in bfloat16 or wider, within the bound.
A program may use at most 192 MiB of HBM per device.

```python
import math
import jax
import jax.numpy as jnp
import numpy as np
from jax import lax

D = 1920
QUERY_HEADS = 8
KEY_VALUE_HEADS = 4
HEAD_SIZE = 256
WINDOW_TOKENS = 1024
BLOCK_TOKENS = 128
TOK_DEV = 128
SEQUENCE_LENGTH = 4096
BATCH_TOTAL = 8
NBLK = 32
DOCS = 8
MOSTB = 8


def draw_query(key, part):
    random_seed_key = jax.random.fold_in(key, 17)
    unmasked_output = jnp.clip(jax.random.normal(random_seed_key, (BATCH_TOTAL, SEQUENCE_LENGTH, QUERY_HEADS * HEAD_SIZE), jnp.float32), -5.0, 5.0)
    return unmasked_output.astype(jnp.bfloat16)


def draw_keys(key, part):
    random_seed_key = jax.random.fold_in(key, 29)
    unmasked_output = jnp.clip(jax.random.normal(random_seed_key, (BATCH_TOTAL, SEQUENCE_LENGTH, KEY_VALUE_HEADS * HEAD_SIZE), jnp.float32), -5.0, 5.0)
    return unmasked_output.astype(jnp.bfloat16)


def steps_of(stream_key, extent, cuts, smallest, high):
    factor_of, own = 1.0, jax.random.fold_in(stream_key, 6)
    for position, shards_of in cuts:
        draws = jnp.exp(jax.random.uniform(jax.random.fold_in(own, position), (shards_of,), jnp.float32, smallest / len(cuts), high / len(cuts)))
        factor_of = factor_of * jnp.repeat(draws, extent[position] // shards_of).reshape([-1 if axis == position else 1 for axis in range(len(extent))])
    return factor_of


def length_profile(number_of, total, limit, slope):
    weights = [(1 << 20) // math.isqrt(grade ** slope) + 1 for grade in range(2, number_of + 1)]
    rest, holding = total - limit - (number_of - 1), [1] * (number_of - 1)
    while rest > 0:
        candidates = [i for i in range(number_of - 1) if holding[i] < limit]
        whole, budget = sum([weights[i] for i in candidates]), rest
        for i in candidates:
            more = min(limit - holding[i], max(1, budget * weights[i] // whole), rest)
            holding[i] = holding[i] + more
            rest = rest - more
    return np.array([limit] + holding)


def uneven(own_key, amount, total, most, lean):
    if amount == 2:
        one = jax.random.randint(own_key, (), max(1, total - most), min(most, total - 1) + 1)
        return jnp.stack([one, total - one])
    sizes = jnp.asarray(length_profile(amount, total, most, lean), jnp.int32)
    twos = (amount - 1) // 2
    donor, sink = sizes[1:1 + 2 * twos:2], sizes[2:2 + 2 * twos:2]
    room = jnp.minimum(donor - 1, most - sink)
    moved = jax.random.randint(jax.random.fold_in(own_key, 1), (twos,), 0, 1 << 20) % (room + 1)
    sizes = sizes.at[1:1 + 2 * twos:2].set(donor - moved).at[2:2 + 2 * twos:2].set(sink + moved)
    return sizes[jax.random.permutation(jax.random.fold_in(own_key, 2), amount)]


def scatter_about(key, shape, spread, reach, cuts=(), kind=jnp.bfloat16):
    drawn = spread * jax.random.normal(key, shape, jnp.float32)
    if cuts:
        drawn = drawn * steps_of(key, shape, cuts, -0.22, 0.18)
    return jnp.clip(drawn, -reach, reach).astype(kind)


def setup_inputs(seed: int = 0) -> dict:
    key_list = jax.random.split(jax.random.key(seed), 7)
    return {
        "query": draw_query(jax.random.fold_in(key_list[6], 71), 0),
        "keys": draw_keys(jax.random.fold_in(key_list[6], 71), 0),
        "values": scatter_about(key_list[2], (BATCH_TOTAL, SEQUENCE_LENGTH, KEY_VALUE_HEADS * HEAD_SIZE), 1.0, 6.0, ((0, 8), (1, 32))),
        "out_weight": scatter_about(key_list[3], (QUERY_HEADS * HEAD_SIZE, D), (QUERY_HEADS * HEAD_SIZE) ** -0.5, 0.125, ((0, 8),)),
        "out_grad": scatter_about(key_list[4], (BATCH_TOTAL, SEQUENCE_LENGTH, D), 1.0, 6.0, ((0, 8), (1, 32))),
        "doc_blocks": jax.vmap(lambda own: uneven(own, DOCS, NBLK, MOSTB, 2))(jax.random.split(key_list[5], BATCH_TOTAL)).reshape((BATCH_TOTAL, DOCS)).astype(jnp.int32),
    }


def one_sequence(items, out_weight):
    query_sequence, key_sequence, value_sequence, grad_seq, lengths = items
    group_total = QUERY_HEADS // KEY_VALUE_HEADS
    scale = HEAD_SIZE ** -0.5
    starts = (jnp.cumsum(lengths) - lengths) * BLOCK_TOKENS
    places = jnp.arange(-WINDOW_TOKENS, SEQUENCE_LENGTH, dtype=jnp.int32)
    docs = jnp.sum((starts[None, :] <= places[:, None]).astype(jnp.int32), axis=1) - 1
    key_padded = jnp.concatenate([jnp.zeros((WINDOW_TOKENS, KEY_VALUE_HEADS * HEAD_SIZE), jnp.bfloat16), key_sequence], axis=0).reshape(WINDOW_TOKENS + SEQUENCE_LENGTH, KEY_VALUE_HEADS, HEAD_SIZE)
    value_padded = jnp.concatenate([jnp.zeros((WINDOW_TOKENS, KEY_VALUE_HEADS * HEAD_SIZE), jnp.bfloat16), value_sequence], axis=0).reshape(WINDOW_TOKENS + SEQUENCE_LENGTH, KEY_VALUE_HEADS, HEAD_SIZE)
    attention_gradient = jnp.dot(grad_seq, out_weight.T, preferred_element_type=jnp.float32).astype(jnp.bfloat16)

    def step(carry, index):
        key_running_sum, value_running_sum = carry
        base_offset = index * BLOCK_TOKENS
        query_tile = lax.dynamic_slice_in_dim(query_sequence, base_offset, BLOCK_TOKENS, 0).reshape(BLOCK_TOKENS, KEY_VALUE_HEADS, group_total, HEAD_SIZE).astype(jnp.float32)
        key_block = lax.dynamic_slice_in_dim(key_padded, base_offset, WINDOW_TOKENS + BLOCK_TOKENS, 0).astype(jnp.float32)
        value_block = lax.dynamic_slice_in_dim(value_padded, base_offset, WINDOW_TOKENS + BLOCK_TOKENS, 0).astype(jnp.float32)
        block_gradient = lax.dynamic_slice_in_dim(attention_gradient, base_offset, BLOCK_TOKENS, 0).reshape(BLOCK_TOKENS, KEY_VALUE_HEADS, group_total, HEAD_SIZE)
        grad_wide = block_gradient.astype(jnp.float32)
        query_place = base_offset + jnp.arange(BLOCK_TOKENS, dtype=jnp.int32)
        key_place = base_offset - WINDOW_TOKENS + jnp.arange(WINDOW_TOKENS + BLOCK_TOKENS, dtype=jnp.int32)
        query_doc = lax.dynamic_slice_in_dim(docs, base_offset + WINDOW_TOKENS, BLOCK_TOKENS, 0)
        key_doc = lax.dynamic_slice_in_dim(docs, base_offset, WINDOW_TOKENS + BLOCK_TOKENS, 0)
        allowed = (key_place[None, :] <= query_place[:, None]) & (key_place[None, :] > query_place[:, None] - WINDOW_TOKENS)
        allowed = allowed & (key_doc[None, :] == query_doc[:, None])
        scores = jnp.einsum("tkgd,ekd->kgte", query_tile, key_block, precision=lax.Precision.HIGHEST) * scale
        masked = jnp.where(allowed, scores, -jnp.inf)
        top = jnp.max(masked, axis=-1, keepdims=True)
        lifted = jnp.where(allowed, jnp.exp(scores - top), 0.0)
        shares = lifted / jnp.sum(lifted, axis=-1, keepdims=True)
        shares_low = shares.astype(jnp.bfloat16)
        shares_wide = shares_low.astype(jnp.float32)
        attn_block = jnp.einsum("kgte,ekd->tkgd", shares_wide, value_block, precision=lax.Precision.HIGHEST).astype(jnp.bfloat16)
        grad_shares = jnp.einsum("tkgd,ekd->kgte", grad_wide, value_block, precision=lax.Precision.HIGHEST)
        centre = jnp.sum(shares * grad_shares, axis=-1, keepdims=True)
        grad_scores = (shares * (grad_shares - centre) * scale).astype(jnp.bfloat16).astype(jnp.float32)
        query_part = jnp.einsum("kgte,ekd->tkgd", grad_scores, key_block, precision=lax.Precision.HIGHEST).astype(jnp.bfloat16)
        key_portion = jnp.einsum("kgte,tkgd->ekd", grad_scores, query_tile, precision=lax.Precision.HIGHEST)
        value_portion = jnp.einsum("kgte,tkgd->ekd", shares_wide, grad_wide, precision=lax.Precision.HIGHEST)
        key_running_sum = lax.dynamic_update_slice_in_dim(key_running_sum, lax.dynamic_slice_in_dim(key_running_sum, base_offset, WINDOW_TOKENS + BLOCK_TOKENS, 0) + key_portion, base_offset, 0)
        value_running_sum = lax.dynamic_update_slice_in_dim(value_running_sum, lax.dynamic_slice_in_dim(value_running_sum, base_offset, WINDOW_TOKENS + BLOCK_TOKENS, 0) + value_portion, base_offset, 0)
        return (key_running_sum, value_running_sum), (attn_block.reshape(BLOCK_TOKENS, QUERY_HEADS * HEAD_SIZE), query_part.reshape(BLOCK_TOKENS, QUERY_HEADS * HEAD_SIZE))

    blank_fill = jnp.zeros((WINDOW_TOKENS + SEQUENCE_LENGTH, KEY_VALUE_HEADS, HEAD_SIZE), jnp.float32)
    (key_running_sum, value_running_sum), (attn_blocks, query_blocks) = lax.scan(step, (blank_fill, blank_fill), jnp.arange(SEQUENCE_LENGTH // BLOCK_TOKENS, dtype=jnp.int32))
    attn = attn_blocks.reshape(SEQUENCE_LENGTH, QUERY_HEADS * HEAD_SIZE)
    layer_out = jnp.dot(attn, out_weight, preferred_element_type=jnp.float32).astype(jnp.bfloat16)
    key_gradient = key_running_sum[WINDOW_TOKENS:].reshape(SEQUENCE_LENGTH, KEY_VALUE_HEADS * HEAD_SIZE).astype(jnp.bfloat16)
    value_gradient = value_running_sum[WINDOW_TOKENS:].reshape(SEQUENCE_LENGTH, KEY_VALUE_HEADS * HEAD_SIZE).astype(jnp.bfloat16)
    return layer_out, query_blocks.reshape(SEQUENCE_LENGTH, QUERY_HEADS * HEAD_SIZE), key_gradient, value_gradient, attn


def reference(query, keys, values, out_weight, out_grad, doc_blocks):
    results = lax.map(lambda items: one_sequence(items, out_weight), (query, keys, values, out_grad, doc_blocks))
    layer_out, query_grad, key_gradient, value_gradient, attn = results
    attn_groups = attn.reshape(BATCH_TOTAL * SEQUENCE_LENGTH // TOK_DEV, TOK_DEV, QUERY_HEADS * HEAD_SIZE)
    grad_groups = out_grad.reshape(BATCH_TOTAL * SEQUENCE_LENGTH // TOK_DEV, TOK_DEV, D)

    def accumulate(total, pair):
        attn_group, grad_group = pair
        term = lax.dot_general(attn_group, grad_group, (((0,), (0,)), ((), ())), preferred_element_type=jnp.float32)
        return total + term, None

    total, unused = lax.scan(accumulate, jnp.zeros((QUERY_HEADS * HEAD_SIZE, D), jnp.float32), (attn_groups, grad_groups))
    weight_grad = total * ((BATCH_TOTAL * SEQUENCE_LENGTH) ** -0.5)
    return layer_out, query_grad, key_gradient, value_gradient, weight_grad
```

```python
import functools

import jax
import jax.numpy as jnp
from jax import lax
from jax.experimental import pallas as pl
from jax.experimental.pallas import tpu as pltpu
from jax.sharding import PartitionSpec as P

HEAD = 256
BLOCK = 128
WINDOW = 1024
SLOTS = 9
ROWS = SLOTS * BLOCK
MESH = pl.DeviceIdType.MESH
F32 = jnp.float32
BF16 = jnp.bfloat16


def device_at(x, y, z, core):
    return (lax.rem(z, 2) * 4 + x, (lax.div(z, 2) * 4 + y) * 2 + core)


def dot(a, b, ca, cb):
    return lax.dot_general(a, b, (((ca,), (cb,)), ((), ())), preferred_element_type=F32)


def kernel(
    normaliser,
    doc_ref, q_ref, k_ref, v_ref, w_ref, og_ref,
    lo_ref, dq_ref, dk_ref, dv_ref, wg_ref,
    own_st, zbuf, win, qh, og_all, w_all, ga_st, ga, bias, shares, attn_loc, attn_all,
    dq_st, dq_rx, dkv, d0_rx, d4_rx, dy_rx, acc, rel_st, dz_rx,
    wg_st, wy_rx, wsum, wz_rx, lp_st, lp_rx, lo_own, lx_st, lx_rx,
    q_sem, og_s, og_r, ogp_s, ogp_r, w_s, w_r, zk_s, zk_r, yk_s, yk_r, pk_s, pk_r, p0_s, p0_r,
    ga_s, ga_r, at_s, at_r, dqs, dqr, d0s, d0r, d4s, d4r, yd_s, yd_r, zd_s, zd_r,
    wy_s, wy_r, wz_s, wz_r, lp_s, lp_r, lx_s, lx_r,
):
    dp = lax.axis_index("dp")
    s = lax.axis_index("seq")
    x, zl = lax.rem(dp, 4), lax.div(dp, 4)
    q, y, zh = lax.rem(s, 2), lax.rem(lax.div(s, 2), 4), lax.div(s, 8)
    z = zh * 2 + zl
    other = 1 - q
    partner = device_at(x, y, z, other)
    scale = HEAD ** (-0.5)

    def mine(i):
        return pl.ds(pl.multiple_of(i * BLOCK, BLOCK), BLOCK)

    def remote(src, dst, ss, rs, dev):
        return pltpu.make_async_remote_copy(
            src_ref=src, dst_ref=dst, send_sem=ss, recv_sem=rs, device_id=dev, device_id_type=MESH
        )

    xs = [lax.rem(x + k, 4) for k in range(4)]
    ys = [lax.rem(y + k, 4) for k in range(4)]

    barrier = pltpu.get_barrier_semaphore()
    count = 0
    for k in range(1, 4):
        pl.semaphore_signal(barrier, 1, device_id=device_at(xs[k], y, z, q), device_id_type=MESH)
        for core in range(2):
            pl.semaphore_signal(
                barrier, 1, device_id=device_at(x, ys[k], z, core), device_id_type=MESH
            )
        count += 3
    pl.semaphore_signal(barrier, 1, device_id=partner, device_id_type=MESH)
    count += 1
    for k in range(1, 8):
        for core in range(2):
            pl.semaphore_signal(
                barrier, 1, device_id=device_at(x, y, lax.rem(z + k, 8), core), device_id_type=MESH
            )
        count += 2

    for half in range(2):
        own_st[half, :, 0:512] = k_ref[:, half * 512 : half * 512 + 512]
        own_st[half, :, 512:1024] = v_ref[:, half * 512 : half * 512 + 512]
    pl.semaphore_wait(barrier, count)

    sends = []

    def go(copy):
        copy.start()
        sends.append(copy)
        return copy

    for half in range(2):
        go(remote(own_st.at[half], zbuf.at[half], zk_s.at[half], zk_r.at[half],
                  device_at(x, y, lax.rem(z + 2, 8), q)))

    def along_y(k, half, src):
        return remote(
            src.at[half], win.at[mine(7 - 2 * k + q)], yk_s.at[k - 1, half], yk_r.at[k - 1, q],
            device_at(x, ys[k], z, half),
        )

    for k in range(1, 4):
        @pl.when(y + k < 4)
        def _():
            for half in range(2):
                along_y(k, half, own_st).start()

    og_cp = {}
    for k in (1, 3, 2):
        og_cp[k] = go(remote(og_ref, og_all.at[4 - k, mine(q)], og_s.at[k], og_r.at[4 - k],
                             device_at(xs[k], y, z, q)))
    go(remote(w_ref.at[mine(q)], w_all.at[mine(q)], w_s, w_r.at[q],
              device_at(x, y, lax.rem(z + 9 - 2 * q, 8), zl)))
    go(remote(own_st.at[other], win.at[mine(7 + q)], pk_s, pk_r, partner))
    go(remote(q_ref.at[:, pl.ds(pl.multiple_of(other * 1024, 1024), 1024)], qh.at[mine(q)],
              q_sem.at[0], q_sem.at[1], partner))
    go(remote(og_ref, og_all.at[0, mine(q)], ogp_s.at[0], ogp_r.at[0], partner))

    win[mine(7 + q), :] = own_st[q]
    qh[mine(q), :] = q_ref[:, pl.ds(pl.multiple_of(q * 1024, 1024), 1024)]
    og_all[0, mine(q), :] = og_ref[...]

    chip = zh * 4 + y
    qp = chip * 256 + lax.broadcasted_iota(jnp.int32, (256, 1), 0)
    kp = (chip * 2 - 7) * BLOCK + lax.broadcasted_iota(jnp.int32, (1, ROWS), 1)
    qd = jnp.zeros((256, 1), jnp.int32)
    kd = jnp.zeros((1, ROWS), jnp.int32)
    start = jnp.int32(0)
    for n in range(8):
        qd = qd + (start <= qp).astype(jnp.int32)
        kd = kd + (start <= kp).astype(jnp.int32)
        start = start + doc_ref[0, n] * BLOCK
    allowed = (kp <= qp) & (kp > qp - WINDOW) & (kd == qd)
    bias[...] = jnp.where(allowed, 0.0, -jnp.inf).astype(F32)

    @pl.when(q == zl)
    def _():
        w_all[...] = w_ref[...]

    def relay(half):
        remote(own_st.at[half], zbuf.at[half], zk_s.at[half], zk_r.at[half], partner).wait_recv()
        for k in range(1, 4):
            @pl.when(y + k >= 4)
            def _():
                along_y(k, half, zbuf).start()

    def og_forward(r):
        og_cp[4 - r].wait_recv()
        go(remote(og_all.at[r, mine(q)], og_all.at[r, mine(q)], ogp_s.at[r], ogp_r.at[r], partner))

    relay(0)
    for r in (1, 3, 2):
        og_forward(r)

    @pl.when(q != zl)
    def _():
        for j in range(2):
            remote(w_ref.at[pl.ds(0, BLOCK)], w_all.at[pl.ds(j * BLOCK, BLOCK)], w_s, w_r.at[j],
                   partner).wait_recv()

    ga_cp = []
    for r in (1, 3, 2, 0):
        remote(og_ref, og_all.at[r, mine(other)], ogp_s.at[r], ogp_r.at[r], partner).wait_recv()
        part = dot(og_all[r], w_all[...], 1, 1).astype(BF16)
        if r == 0:
            ga[x] = part
        else:
            ga_st[r - 1] = part
            ga_cp.append(go(remote(ga_st.at[r - 1], ga.at[x], ga_s.at[r - 1], ga_r.at[r - 1],
                                   device_at(xs[r], y, z, q))))
    relay(1)

    @pl.when(q == 1)
    def _():
        remote(zbuf.at[0], win.at[pl.ds(0, BLOCK)], p0_s, p0_r, partner).start()
        win[0:BLOCK, :] = zbuf[1]

    remote(own_st.at[0], win.at[mine(7 + other)], pk_s, pk_r, partner).wait_recv()
    remote(q_ref.at[:, pl.ds(0, 1024)], qh.at[mine(other)], q_sem.at[0], q_sem.at[1],
           partner).wait_recv()
    for k in range(1, 4):
        for j in range(2):
            remote(own_st.at[0], win.at[mine(7 - 2 * k + j)], yk_s.at[k - 1, 0], yk_r.at[k - 1, j],
                   partner).wait_recv()

    @pl.when(q == 0)
    def _():
        remote(zbuf.at[0], win.at[pl.ds(0, BLOCK)], p0_s, p0_r, partner).wait_recv()

    def lanes(i):
        return pl.ds(pl.multiple_of(i * HEAD, HEAD), HEAD)

    def forward(h, carry):
        m = lax.div(h, 2)
        scores = dot(qh[:, lanes(h)], win[:, lanes(m)], 1, 1) * scale + bias[...]
        top = jnp.max(scores, axis=-1, keepdims=True)
        lifted = jnp.exp(scores - top)
        share = lifted * (1.0 / jnp.sum(lifted, axis=-1, keepdims=True))
        shares[h] = share
        attn_loc[h] = dot(share.astype(BF16), win[:, lanes(m + 2)], 1, 0).astype(BF16)
        return carry

    lax.fori_loop(0, 4, forward, 0)

    at_cp = []
    for k in (1, 3, 2):
        at_cp.append(go(remote(attn_loc.at[xs[k]], attn_all.at[4 - k], at_s.at[k - 1],
                               at_r.at[k - 1], device_at(xs[k], y, z, q))))
    attn_all[0] = attn_loc[x]

    for copy in ga_cp:
        copy.wait_recv()

    def backward(m, carry):
        dk = jnp.zeros((ROWS, HEAD), F32)
        dv = jnp.zeros((ROWS, HEAD), F32)
        for g in range(2):
            h = m * 2 + g
            share = shares[h]
            gh = ga[h]
            gs = dot(gh, win[:, lanes(m + 2)], 1, 1)
            centre = jnp.sum(share * gs, axis=-1, keepdims=True)
            ds = (share * (gs - centre) * scale).astype(BF16)
            dq_st[h] = dot(ds, win[:, lanes(m)], 1, 0).astype(BF16)
            dk = dk + dot(ds, qh[:, lanes(h)], 0, 0)
            dv = dv + dot(share.astype(BF16), gh, 0, 0)
        dkv[:, lanes(m)] = dk.astype(BF16)
        dkv[:, lanes(m + 2)] = dv.astype(BF16)
        return carry

    lax.fori_loop(0, 2, backward, 0)

    yd_cp = {}
    for k in (3, 2, 1):
        for j in range(2):
            yd_cp[k, j] = go(remote(
                dkv.at[pl.ds((7 - 2 * k + j) * BLOCK, BLOCK)], dy_rx.at[k - 1, q],
                yd_s.at[k - 1, j], yd_r.at[k - 1, q], device_at(x, ys[4 - k], z, j)))

    @pl.when(q == 0)
    def _():
        remote(dkv.at[pl.ds(0, BLOCK)], d4_rx, d4s, d4r, partner).start()

    go(remote(dkv.at[mine(7 + other)], d0_rx, d0s, d0r, partner))
    go(remote(dq_st.at[:, mine(other)], dq_rx, dqs, dqr, partner))

    for copy in at_cp:
        copy.wait_recv()
    lp_cp = []
    for r in (1, 3, 2, 0):
        lp_st[r] = dot(attn_all[r, mine(other), :], w_all[...], 1, 0).astype(BF16)
        lp_cp.append(go(remote(lp_st.at[r], lp_rx.at[r], lp_s.at[r], lp_r.at[r], partner)))
        lo_own[r] = dot(attn_all[r, mine(q), :], w_all[...], 1, 0)

    acc[...] = jnp.zeros_like(acc)

    def dy_wait(k):
        for half in range(2):
            remote(own_st.at[0], dy_rx.at[k - 1, half], yd_s.at[0, 0], yd_r.at[k - 1, half],
                   partner).wait_recv()

    @pl.when(q == 1)
    def _():
        remote(own_st.at[0], d4_rx, d4s, d4r, partner).wait_recv()
        acc[0] = d4_rx[...].astype(F32)
        acc[1] = dkv[0:BLOCK, :].astype(F32)

    for k in (3, 2, 1):
        @pl.when(y + k >= 4)
        def _():
            dy_wait(k)
            acc[...] += dy_rx[k - 1].astype(F32)
    for half in range(2):
        rel_st[half] = acc[half].astype(BF16)
        go(remote(rel_st.at[half], dz_rx.at[half], zd_s.at[half], zd_r.at[half],
                  device_at(x, y, lax.rem(z + 6, 8), q)))

    lx_cp = []
    for i, r in enumerate((1, 3, 2)):
        lp_cp[i].wait_recv()
        lx_st[r - 1] = (lo_own[r] + lp_rx[r].astype(F32)).astype(BF16)
        lx_cp.append(go(remote(lx_st.at[r - 1], lx_rx.at[r - 1], lx_s.at[r - 1], lx_r.at[r - 1],
                               device_at(xs[r], y, z, q))))
    lp_cp[3].wait_recv()

    product = dot(attn_all[...].reshape(1024, HEAD), og_all[...].reshape(1024, og_ref.shape[1]), 0, 0)
    for yy in range(4):
        for zz in range(4):
            wg_st[yy, zz * 16 : zz * 16 + 16, :] = product[
                (zz * 4 + yy) * 16 : (zz * 4 + yy) * 16 + 16, :
            ].astype(BF16)
    wy_cp = []
    for k in (1, 3, 2):
        wy_cp.append(go(remote(wg_st.at[ys[k]], wy_rx.at[k - 1], wy_s.at[k - 1], wy_r.at[k - 1],
                               device_at(x, ys[k], z, q))))

    dq_mine = dq_st[:, mine(q), :]
    remote(dq_rx, dq_rx, dqs, dqr, partner).wait_recv()
    for h in range(4):
        dq_ref[:, lanes(q * 4 + h)] = dq_mine[h]
        dq_ref[:, lanes(other * 4 + h)] = dq_rx[h]

    for copy in wy_cp:
        copy.wait_recv()
    total = wg_st[y].astype(F32)
    for k in range(3):
        total = total + wy_rx[k].astype(F32)
    wsum[...] = total.reshape(8, 8, total.shape[-1])

    def to_z(i):
        return remote(wsum.at[i], wz_rx.at[z], wz_s.at[i], wz_r.at[z],
                      device_at(x, y, (i // 2) * 2 + q, i % 2))

    for i in range(8):
        here = ((i // 2) * 2 + q == z) & (q == i % 2)

        @pl.when(jnp.logical_not(here))
        def _():
            to_z(i).start()

        @pl.when(here)
        def _():
            wz_rx[z] = wsum[i]

    out = lo_own[0] + lp_rx[0].astype(F32)
    for i, r in enumerate((1, 3, 2)):
        lx_cp[i].wait_recv()
        out = out + lx_rx[r - 1].astype(F32)
    lo_ref[...] = out.astype(BF16)

    remote(own_st.at[0], d0_rx, d0s, d0r, partner).wait_recv()
    acc[q] = dkv[mine(7 + q), :].astype(F32)
    acc[other] = d0_rx[...].astype(F32)
    for k in (3, 2, 1):
        @pl.when(y + k < 4)
        def _():
            dy_wait(k)
            acc[...] += dy_rx[k - 1].astype(F32)
    for half in range(2):
        remote(rel_st.at[half], dz_rx.at[half], zd_s.at[half], zd_r.at[half], partner).wait_recv()
        own = (acc[half] + dz_rx[half].astype(F32)).astype(BF16)
        dk_ref[:, half * 512 : half * 512 + 512] = own[:, 0:512]
        dv_ref[:, half * 512 : half * 512 + 512] = own[:, 512:1024]

    for src in range(8):
        here = (z == src) & (zl == q)

        @pl.when(jnp.logical_not(here))
        def _():
            remote(wsum.at[0], wz_rx.at[src], wz_s.at[0], wz_r.at[src], partner).wait_recv()

    wg_ref[...] = jnp.sum(wz_rx[...], axis=0) * normaliser

    for copy in sends:
        copy.wait_send()
    for k in range(1, 4):
        for half in range(2):
            along_y(k, half, own_st).wait_send()
    for i in range(8):
        here = ((i // 2) * 2 + q == z) & (q == i % 2)

        @pl.when(jnp.logical_not(here))
        def _():
            to_z(i).wait_send()

    @pl.when(q == 1)
    def _():
        remote(zbuf.at[0], win.at[pl.ds(0, BLOCK)], p0_s, p0_r, partner).wait_send()

    @pl.when(q == 0)
    def _():
        remote(dkv.at[pl.ds(0, BLOCK)], d4_rx, d4s, d4r, partner).wait_send()


def per_device(query, keys, values, out_weight, out_grad, doc_blocks):
    width = out_grad.shape[2]
    tokens = lax.axis_size("dp") * lax.axis_size("seq") * BLOCK
    vmem = pl.BlockSpec(memory_space=pltpu.VMEM)
    dma = pltpu.SemaphoreType.DMA
    scratch = [
        ((2, BLOCK, 1024), BF16),
        ((2, BLOCK, 1024), BF16),
        ((ROWS, 1024), BF16),
        ((256, 1024), BF16),
        ((4, 256, width), BF16),
        ((HEAD, width), BF16),
        ((3, 256, HEAD), BF16),
        ((4, 256, HEAD), BF16),
        ((256, ROWS), F32),
        ((4, 256, ROWS), F32),
        ((4, 256, HEAD), BF16),
        ((4, 256, HEAD), BF16),
        ((4, 256, HEAD), BF16),
        ((4, BLOCK, HEAD), BF16),
        ((ROWS, 1024), BF16),
        ((BLOCK, 1024), BF16),
        ((BLOCK, 1024), BF16),
        ((3, 2, BLOCK, 1024), BF16),
        ((2, BLOCK, 1024), F32),
        ((2, BLOCK, 1024), BF16),
        ((2, BLOCK, 1024), BF16),
        ((4, 64, width), BF16),
        ((3, 64, width), BF16),
        ((8, 8, width), F32),
        ((8, 8, width), F32),
        ((4, BLOCK, width), BF16),
        ((4, BLOCK, width), BF16),
        ((4, BLOCK, width), F32),
        ((3, BLOCK, width), BF16),
        ((3, BLOCK, width), BF16),
    ]
    semaphores = [
        (2,), (4,), (4,), (4,), (4,), (), (2,), (2,), (2,), (3, 2), (3, 2), (), (), (), (),
        (3,), (3,), (3,), (3,), (), (), (), (), (), (), (3, 2), (3, 2), (2,), (2,),
        (3,), (3,), (8,), (8,), (4,), (4,), (3,), (3,),
    ]
    layer_out, query_grad, key_gradient, value_gradient, weight_grad = pl.pallas_call(
        functools.partial(kernel, tokens ** (-0.5)),
        out_shape=[
            jax.ShapeDtypeStruct((BLOCK, width), BF16),
            jax.ShapeDtypeStruct((BLOCK, 2048), BF16),
            jax.ShapeDtypeStruct((BLOCK, 1024), BF16),
            jax.ShapeDtypeStruct((BLOCK, 1024), BF16),
            jax.ShapeDtypeStruct((8, width), F32),
        ],
        in_specs=[pl.BlockSpec(memory_space=pltpu.SMEM)] + [vmem] * 5,
        out_specs=[vmem] * 5,
        scratch_shapes=[pltpu.VMEM(*a) for a in scratch]
        + [dma(a) if a else dma for a in semaphores],
        compiler_params=pltpu.CompilerParams(
            collective_id=0, has_side_effects=True, vmem_limit_bytes=60 << 20
        ),
    )(doc_blocks, query[0], keys[0], values[0], out_weight, out_grad[0])
    return (
        layer_out[None],
        query_grad[None],
        key_gradient[None],
        value_gradient[None],
        weight_grad,
    )


def solution(mesh):
    tokens = P("dp", "seq", None)
    return jax.shard_map(
        per_device,
        mesh=mesh,
        in_specs=(tokens, tokens, tokens, P("dp", None), tokens, P("dp", None)),
        out_specs=(tokens, tokens, tokens, tokens, P(("dp", "seq"), None)),
        check_vma=False,
    )
```

```python
import functools

import jax
import jax.numpy as jnp
from jax import lax
from jax.experimental import pallas as pl
from jax.experimental.pallas import tpu as pltpu
from jax.sharding import PartitionSpec as P

HEAD = 256
BLOCK = 128
WINDOW = 1024
SLOTS = 9
ROWS = SLOTS * BLOCK
SPLIT = 1152
MESH = pl.DeviceIdType.MESH
F32 = jnp.float32
BF16 = jnp.bfloat16


def device_at(x, y, z, core):
    return (lax.rem(z, 2) * 4 + x, (lax.div(z, 2) * 4 + y) * 2 + core)


def dot(a, b, ca, cb):
    return lax.dot_general(a, b, (((ca,), (cb,)), ((), ())), preferred_element_type=F32)


def kernel(
    normaliser,
    doc_ref, q_ref, k_ref, v_ref, w_ref, og_ref,
    lo_ref, dq_ref, dk_ref, dv_ref, wg_ref,
    own_st, zbuf, win, qh, og_all, w_all, ga_st, ga, bias, shares, attn_loc, attn_all,
    dq_st, dq_rx, dkv, d0_rx, d4_rx, dy_rx, acc, rel_st, dz_rx,
    wg_st, wy_rx, wsum, wz_rx, wp_st, wp_rx, lp_st, lp_rx, lo_own, lx_st, lx_rx, wx, lt_st, lt_rx, lt_own,
    q_sem, og_s, og_r, ogp_s, ogp_r, w_s, w_r, zk_s, zk_r, yk_s, yk_r, pk_s, pk_r, p0_s, p0_r,
    ga_s, ga_r, at_s, at_r, dqs, dqr, d0s, d0r, d4s, d4r, yd_s, yd_r, zd_s, zd_r,
    wy_s, wy_r, wz_s, wz_r, wp_s, wp_r, lp_s, lp_r, lx_s, lx_r,
    wx_s, wx_r, lt_s, lt_r,
):
    dp = lax.axis_index("dp")
    s = lax.axis_index("seq")
    x, zl = lax.rem(dp, 4), lax.div(dp, 4)
    q, y, zh = lax.rem(s, 2), lax.rem(lax.div(s, 2), 4), lax.div(s, 8)
    z = zh * 2 + zl
    other = 1 - q
    partner = device_at(x, y, z, other)
    scale = HEAD ** (-0.5)
    split = SPLIT

    def mine(i):
        return pl.ds(pl.multiple_of(i * BLOCK, BLOCK), BLOCK)

    def remote(src, dst, ss, rs, dev):
        return pltpu.make_async_remote_copy(
            src_ref=src, dst_ref=dst, send_sem=ss, recv_sem=rs, device_id=dev, device_id_type=MESH
        )

    xs = [lax.rem(x + k, 4) for k in range(4)]
    ys = [lax.rem(y + k, 4) for k in range(4)]

    barrier = pltpu.get_barrier_semaphore()
    count = 0
    for k in range(1, 4):
        pl.semaphore_signal(barrier, 1, device_id=device_at(xs[k], y, z, q), device_id_type=MESH)
        for core in range(2):
            pl.semaphore_signal(
                barrier, 1, device_id=device_at(x, ys[k], z, core), device_id_type=MESH
            )
        count += 3
    pl.semaphore_signal(barrier, 1, device_id=partner, device_id_type=MESH)
    count += 1
    for k in range(1, 8):
        for core in range(2):
            pl.semaphore_signal(
                barrier, 1, device_id=device_at(x, y, lax.rem(z + k, 8), core), device_id_type=MESH
            )
        count += 2

    for half in range(2):
        for m in range(2):
            lo = half * 512 + m * HEAD
            own_st[m, half, :, 0:HEAD] = k_ref[:, lo : lo + HEAD]
            own_st[m, half, :, HEAD : 2 * HEAD] = v_ref[:, lo : lo + HEAD]
    pl.semaphore_wait(barrier, count)

    sends = []

    def go(copy):
        copy.start()
        sends.append(copy)
        return copy

    def up_z(m):
        return remote(own_st.at[m], zbuf.at[m], zk_s.at[m], zk_r.at[m],
                      device_at(x, y, lax.rem(z + 2, 8), q))

    def along_y(m, k, half, src):
        return remote(
            src.at[m, half], win.at[m, mine(7 - 2 * k + q)], yk_s.at[m, k - 1, half],
            yk_r.at[m, k - 1, q], device_at(x, ys[k], z, half),
        )

    def og_send(k):
        return go(remote(og_ref, og_all.at[4 - k, mine(q)], og_s.at[k], og_r.at[4 - k],
                         device_at(xs[k], y, z, q)))

    up_z(0).start()
    up_z(1).start()
    og_cp = {1: og_send(1), 3: og_send(3)}
    for m in range(2):
        for k in range(1, 4):
            @pl.when(y + k < 4)
            def _():
                for half in range(2):
                    along_y(m, k, half, own_st).start()

    go(remote(w_ref.at[mine(q)], w_all.at[mine(q)], w_s, w_r.at[q],
              device_at(x, y, lax.rem(z + 7, 8), zl)))
    go(remote(og_ref, og_all.at[0, mine(q)], ogp_s.at[0], ogp_r.at[0], partner))
    for m in range(2):
        go(remote(own_st.at[m, other], win.at[m, mine(7 + q)], pk_s.at[m], pk_r.at[m], partner))
    go(remote(q_ref.at[:, pl.ds(pl.multiple_of(other * 1024, 1024), 1024)], qh.at[mine(q)],
              q_sem.at[0], q_sem.at[1], partner))

    for m in range(2):
        win[m, mine(7 + q), :] = own_st[m, q]
    qh[mine(q), :] = q_ref[:, pl.ds(pl.multiple_of(q * 1024, 1024), 1024)]
    og_all[0, mine(q), :] = og_ref[...]

    chip = zh * 4 + y
    qp = chip * 256 + lax.broadcasted_iota(jnp.int32, (256, 1), 0)
    kp = (chip * 2 - 7) * BLOCK + lax.broadcasted_iota(jnp.int32, (1, ROWS), 1)
    qd = jnp.zeros((256, 1), jnp.int32)
    kd = jnp.zeros((1, ROWS), jnp.int32)
    start = jnp.int32(0)
    for n in range(8):
        qd = qd + (start <= qp).astype(jnp.int32)
        kd = kd + (start <= kp).astype(jnp.int32)
        start = start + doc_ref[0, n] * BLOCK
    allowed = (kp <= qp) & (kp > qp - WINDOW) & (kd == qd)
    bias[...] = jnp.where(allowed, 0.0, -jnp.inf).astype(F32)

    @pl.when(q == zl)
    def _():
        w_all[...] = w_ref[...]

    def relay(m):
        up_z(m).wait_recv()
        for k in range(1, 4):
            @pl.when(y + k >= 4)
            def _():
                for half in range(2):
                    along_y(m, k, half, zbuf).start()

        @pl.when(q == 1)
        def _():
            remote(zbuf.at[m, 0], win.at[m, pl.ds(0, BLOCK)], p0_s.at[m], p0_r.at[m],
                   partner).start()
            win[m, 0:BLOCK, :] = zbuf[m, 1]

    def og_forward(r):
        og_cp[4 - r].wait_recv()
        go(remote(og_all.at[r, mine(q)], og_all.at[r, mine(q)], ogp_s.at[r], ogp_r.at[r], partner))

    def head_gradient(r):
        remote(og_ref, og_all.at[r, mine(other)], ogp_s.at[r], ogp_r.at[r], partner).wait_recv()
        part = dot(og_all[r], w_all[...], 1, 1).astype(BF16)
        if r == 0:
            ga[x] = part
        else:
            ga_st[r - 1] = part
            go(remote(ga_st.at[r - 1], ga.at[x], ga_s.at[r - 1], ga_r.at[x],
                      device_at(xs[r], y, z, q)))

    def window_wait(m):
        remote(own_st.at[0, 0], win.at[m, mine(7 + other)], pk_s.at[m], pk_r.at[m],
               partner).wait_recv()
        for k in range(1, 4):
            for j in range(2):
                remote(own_st.at[0, 0], win.at[m, mine(7 - 2 * k + j)], yk_s.at[m, 0, 0],
                       yk_r.at[m, k - 1, j], partner).wait_recv()

        @pl.when(q == 0)
        def _():
            remote(zbuf.at[m, 0], win.at[m, pl.ds(0, BLOCK)], p0_s.at[m], p0_r.at[m],
                   partner).wait_recv()

    def lanes(i):
        return pl.ds(pl.multiple_of(i * HEAD, HEAD), HEAD)

    def attn_copy(h):
        r = lax.rem(x - h + 4, 4)
        return remote(attn_loc.at[h], attn_all.at[r], at_s.at[h], at_r.at[r],
                      device_at(jnp.int32(h), y, z, q))

    def forward(m):
        for g in range(2):
            h = m * 2 + g
            scores = dot(qh[:, h * HEAD : h * HEAD + HEAD], win[m, :, 0:HEAD], 1, 1) * scale
            scores = scores + bias[...]
            top = jnp.max(scores, axis=-1, keepdims=True)
            lifted = jnp.exp(scores - top)
            share = lifted * (1.0 / jnp.sum(lifted, axis=-1, keepdims=True))
            shares[g] = share
            attn_loc[h] = dot(share.astype(BF16), win[m, :, HEAD:], 1, 0).astype(BF16)

            @pl.when(x != h)
            def _():
                attn_copy(h).start()

            @pl.when(x == h)
            def _():
                attn_all[0] = attn_loc[h]

    def dy_copy(m, k, j):
        return remote(
            dkv.at[m, pl.ds((7 - 2 * k + j) * BLOCK, BLOCK)], dy_rx.at[m, k - 1, q],
            yd_s.at[m, k - 1, j], yd_r.at[m, k - 1, q], device_at(x, ys[4 - k], z, j))

    def backward(m):
        dk = jnp.zeros((ROWS, HEAD), F32)
        dv = jnp.zeros((ROWS, HEAD), F32)
        for g in range(2):
            h = m * 2 + g

            @pl.when(x != h)
            def _():
                remote(ga_st.at[0], ga.at[h], ga_s.at[0], ga_r.at[h], partner).wait_recv()

            share = shares[g]
            gh = ga[h]
            gs = dot(gh, win[m, :, HEAD:], 1, 1)
            centre = jnp.sum(share * gs, axis=-1, keepdims=True)
            ds = (share * (gs - centre) * scale).astype(BF16)
            dq_st[h] = dot(ds, win[m, :, 0:HEAD], 1, 0).astype(BF16)
            dk = dk + dot(ds, qh[:, h * HEAD : h * HEAD + HEAD], 0, 0)
            dv = dv + dot(share.astype(BF16), gh, 0, 0)
        dkv[m, :, 0:HEAD] = dk.astype(BF16)
        dkv[m, :, HEAD:] = dv.astype(BF16)

        for k in (3, 2, 1):
            for j in range(2):
                go(dy_copy(m, k, j))

        @pl.when(q == 0)
        def _():
            remote(dkv.at[m, pl.ds(0, BLOCK)], d4_rx.at[m], d4s.at[m], d4r.at[m], partner).start()

        go(remote(dkv.at[m, mine(7 + other)], d0_rx.at[m], d0s.at[m], d0r.at[m], partner))

    def dy_add(m, k):
        for half in range(2):
            remote(own_st.at[0, 0], dy_rx.at[m, k - 1, half], yd_s.at[0, 0, 0],
                   yd_r.at[m, k - 1, half], partner).wait_recv()
        acc[m] += dy_rx[m, k - 1].astype(F32)

    def down_z(m):
        return remote(rel_st.at[m], dz_rx.at[m], zd_s.at[m], zd_r.at[m],
                      device_at(x, y, lax.rem(z + 6, 8), q))

    def relay_sums(m):
        acc[m] = jnp.zeros_like(acc[m])

        @pl.when(q == 1)
        def _():
            remote(own_st.at[0, 0], d4_rx.at[m], d4s.at[m], d4r.at[m], partner).wait_recv()
            acc[m, 0] = d4_rx[m].astype(F32)
            acc[m, 1] = dkv[m, 0:BLOCK, :].astype(F32)

        for k in (3, 2, 1):
            @pl.when(y + k >= 4)
            def _():
                dy_add(m, k)
        rel_st[m] = acc[m].astype(BF16)
        go(down_z(m))

    def own_sums(m):
        remote(own_st.at[0, 0], d0_rx.at[m], d0s.at[m], d0r.at[m], partner).wait_recv()
        acc[m, q] = dkv[m, mine(7 + q), :].astype(F32)
        acc[m, other] = d0_rx[m].astype(F32)
        for k in (3, 2, 1):
            @pl.when(y + k < 4)
            def _():
                dy_add(m, k)

    def own_finish(m):
        down_z(m).wait_recv()
        for half in range(2):
            own = (acc[m, half] + dz_rx[m, half].astype(F32)).astype(BF16)
            lo = half * 512 + m * HEAD
            dk_ref[:, lo : lo + HEAD] = own[:, 0:HEAD]
            dv_ref[:, lo : lo + HEAD] = own[:, HEAD:]

    def weight_wait():
        @pl.when(q != zl)
        def _():
            for j in range(2):
                remote(w_ref.at[pl.ds(0, BLOCK)], w_all.at[pl.ds(j * BLOCK, BLOCK)], w_s,
                       w_r.at[j], partner).wait_recv()

    def query_wait():
        remote(q_ref.at[:, pl.ds(0, 1024)], qh.at[mine(other)], q_sem.at[0], q_sem.at[1],
               partner).wait_recv()

    def attn_wait():
        for r in (1, 3, 2):
            remote(attn_loc.at[0], attn_all.at[r], at_s.at[0], at_r.at[r], partner).wait_recv()

    def wx_copy(k):
        return remote(w_all.at[:, split:], wx.at[x], wx_s.at[k - 1], wx_r.at[x],
                      device_at(xs[k], y, z, q))

    def wx_send():
        wx[x] = w_all[:, split:]
        for k in (1, 3, 2):
            go(wx_copy(k))

    def tail_copy():
        return remote(lt_st, lt_rx, lt_s, lt_r, partner)

    def tail_product():
        for h in range(4):
            @pl.when(x != h)
            def _():
                remote(wx.at[0], wx.at[h], wx_s.at[0], wx_r.at[h], partner).wait_recv()

        lt_st[...] = sum(dot(attn_loc[h, mine(other), :], wx[h], 1, 0) for h in range(4))
        go(tail_copy())
        lt_own[...] = sum(dot(attn_loc[h, mine(q), :], wx[h], 1, 0) for h in range(4))

    def tail_finish():
        tail_copy().wait_recv()
        lo_ref[:, split:] = (lt_own[...] + lt_rx[...]).astype(BF16)

    def lo_pair(r):
        return remote(lp_st.at[r], lp_rx.at[r], lp_s.at[r], lp_r.at[r], partner)

    def lo_product(r):
        lp_st[r] = dot(attn_all[r, mine(other), :], w_all[:, 0:split], 1, 0).astype(BF16)
        go(lo_pair(r))
        lo_own[r] = dot(attn_all[r, mine(q), :], w_all[:, 0:split], 1, 0)

    def lo_copy(r):
        return remote(lx_st.at[r - 1], lx_rx.at[r - 1], lx_s.at[r - 1], lx_r.at[r - 1],
                      device_at(xs[r], y, z, q))

    def lo_send(r):
        lo_pair(r).wait_recv()
        lx_st[r - 1] = (lo_own[r] + lp_rx[r].astype(F32)).astype(BF16)
        go(lo_copy(r))

    def lo_finish():
        lo_pair(0).wait_recv()
        out = lo_own[0] + lp_rx[0].astype(F32)
        for r in (1, 3, 2):
            lo_copy(r).wait_recv()
            out = out + lx_rx[r - 1].astype(F32)
        lo_ref[:, 0:split] = out.astype(BF16)

    def wy_copy(k):
        return remote(wg_st.at[ys[k]], wy_rx.at[k - 1], wy_s.at[k - 1], wy_r.at[k - 1],
                      device_at(x, ys[k], z, q))

    def wg_product():
        product = dot(attn_all[...].reshape(1024, HEAD),
                      og_all[...].reshape(1024, og_ref.shape[1]), 0, 0)
        for yy in range(4):
            for zz in range(4):
                wg_st[yy, zz * 16 : zz * 16 + 16, :] = product[
                    (zz * 4 + yy) * 16 : (zz * 4 + yy) * 16 + 16, :
                ].astype(BF16)
        for k in (1, 3, 2):
            go(wy_copy(k))

    def to_z(i):
        return remote(wsum.at[i], wz_rx.at[zh], wz_s.at[i], wz_r.at[zh],
                      device_at(x, y, i * 2 + q, zl))

    def wg_rows():
        total = wg_st[y].astype(F32)
        for k in (1, 3, 2):
            wy_copy(k).wait_recv()
            total = total + wy_rx[k - 1].astype(F32)
        wsum[...] = total.astype(BF16).reshape(4, 16, total.shape[-1])
        for i in range(4):
            here = (i == zh) & (zl == q)

            @pl.when(jnp.logical_not(here))
            def _():
                to_z(i).start()

            @pl.when(here)
            def _():
                wz_rx[zh] = wsum[i]

    def wp_copy():
        return remote(wp_st.at[other], wp_rx, wp_s, wp_r, partner)

    def wg_swap():
        for i in range(4):
            here = (i == zh) & (zl == q)

            @pl.when(jnp.logical_not(here))
            def _():
                remote(wsum.at[0], wz_rx.at[i], wz_s.at[0], wz_r.at[i], partner).wait_recv()

        rows = jnp.sum(wz_rx[...].astype(F32), axis=0)
        wp_st[...] = rows.reshape(2, 8, rows.shape[-1])
        go(wp_copy())

    def wg_finish():
        wp_copy().wait_recv()
        wg_ref[...] = (wp_st[q] + wp_rx[...]) * normaliser

    def dq_copy():
        return remote(dq_st.at[:, mine(other)], dq_rx, dqs, dqr, partner)

    def dq_finish():
        dq_mine = dq_st[:, mine(q), :]
        dq_copy().wait_recv()
        for h in range(4):
            dq_ref[:, lanes(q * 4 + h)] = dq_mine[h]
            dq_ref[:, lanes(other * 4 + h)] = dq_rx[h]

    og_forward(1)
    og_forward(3)
    og_far = 3 - 2 * q
    og_cp[2] = go(remote(og_all.at[og_far, mine(q)], og_all.at[2, mine(q)], og_s.at[2],
                         og_r.at[2], device_at(lax.rem(x + 5 - 2 * q, 4), y, z, q)))
    relay(0)
    weight_wait()
    head_gradient(1)
    head_gradient(3)
    head_gradient(0)
    query_wait()
    og_forward(2)
    head_gradient(2)
    wx_send()
    window_wait(0)
    forward(0)
    relay(1)
    backward(0)
    window_wait(1)
    forward(1)
    relay_sums(0)
    backward(1)
    go(dq_copy())
    attn_wait()
    wg_product()
    for r in (1, 3, 2, 0):
        lo_product(r)
    for r in (1, 3, 2):
        lo_send(r)
    relay_sums(1)
    tail_product()
    dq_finish()
    own_sums(0)
    own_sums(1)
    wg_rows()
    tail_finish()
    wg_swap()
    lo_finish()
    own_finish(0)
    wg_finish()
    own_finish(1)

    for copy in sends:
        copy.wait_send()
    up_z(0).wait_send()
    up_z(1).wait_send()
    for m in range(2):
        for k in range(1, 4):
            for half in range(2):
                along_y(m, k, half, own_st).wait_send()
    for h in range(4):
        @pl.when(x != h)
        def _():
            attn_copy(h).wait_send()
    for i in range(4):
        @pl.when(jnp.logical_not((i == zh) & (zl == q)))
        def _():
            to_z(i).wait_send()

    for m in range(2):
        @pl.when(q == 1)
        def _():
            remote(zbuf.at[m, 0], win.at[m, pl.ds(0, BLOCK)], p0_s.at[m], p0_r.at[m],
                   partner).wait_send()

        @pl.when(q == 0)
        def _():
            remote(dkv.at[m, pl.ds(0, BLOCK)], d4_rx.at[m], d4s.at[m], d4r.at[m],
                   partner).wait_send()


def hand_over(*refs):
    for src, dst in zip(refs[:5], refs[5:]):
        dst[...] = src[...]


def per_device(query, keys, values, out_weight, out_grad, doc_blocks):
    width = out_grad.shape[2]
    tokens = lax.axis_size("dp") * lax.axis_size("seq") * BLOCK
    vmem = pl.BlockSpec(memory_space=pltpu.VMEM)
    dma = pltpu.SemaphoreType.DMA
    scratch = [
        ((2, 2, BLOCK, 512), BF16),
        ((2, 2, BLOCK, 512), BF16),
        ((2, ROWS, 512), BF16),
        ((256, 1024), BF16),
        ((4, 256, width), BF16),
        ((HEAD, width), BF16),
        ((3, 256, HEAD), BF16),
        ((4, 256, HEAD), BF16),
        ((256, ROWS), F32),
        ((2, 256, ROWS), F32),
        ((4, 256, HEAD), BF16),
        ((4, 256, HEAD), BF16),
        ((4, 256, HEAD), BF16),
        ((4, BLOCK, HEAD), BF16),
        ((2, ROWS, 512), BF16),
        ((2, BLOCK, 512), BF16),
        ((2, BLOCK, 512), BF16),
        ((2, 3, 2, BLOCK, 512), BF16),
        ((2, 2, BLOCK, 512), F32),
        ((2, 2, BLOCK, 512), BF16),
        ((2, 2, BLOCK, 512), BF16),
        ((4, 64, width), BF16),
        ((3, 64, width), BF16),
        ((4, 16, width), BF16),
        ((4, 16, width), BF16),
        ((2, 8, width), F32),
        ((8, width), F32),
        ((4, BLOCK, SPLIT), BF16),
        ((4, BLOCK, SPLIT), BF16),
        ((4, BLOCK, SPLIT), F32),
        ((3, BLOCK, SPLIT), BF16),
        ((3, BLOCK, SPLIT), BF16),
        ((4, HEAD, width - SPLIT), BF16),
        ((BLOCK, width - SPLIT), F32),
        ((BLOCK, width - SPLIT), F32),
        ((BLOCK, width - SPLIT), F32),
    ]
    semaphores = [
        (2,), (4,), (4,), (4,), (4,), (), (2,), (2,), (2,), (2, 3, 2), (2, 3, 2),
        (2,), (2,), (2,), (2,), (3,), (4,), (4,), (4,), (), (), (2,), (2,), (2,), (2,),
        (2, 3, 2), (2, 3, 2), (2,), (2,),
        (3,), (3,), (4,), (4,), (), (), (4,), (4,), (3,), (3,),
        (3,), (4,), (), (),
    ]
    results = pl.pallas_call(
        functools.partial(kernel, tokens ** (-0.5)),
        out_shape=[
            jax.ShapeDtypeStruct((BLOCK, width), BF16),
            jax.ShapeDtypeStruct((BLOCK, 2048), BF16),
            jax.ShapeDtypeStruct((BLOCK, 1024), BF16),
            jax.ShapeDtypeStruct((BLOCK, 1024), BF16),
            jax.ShapeDtypeStruct((8, width), F32),
        ],
        in_specs=[pl.BlockSpec(memory_space=pltpu.SMEM)] + [vmem] * 5,
        out_specs=[vmem] * 5,
        scratch_shapes=[pltpu.VMEM(*a) for a in scratch]
        + [dma(a) if a else dma for a in semaphores],
        compiler_params=pltpu.CompilerParams(
            collective_id=0, has_side_effects=True, vmem_limit_bytes=60 << 20
        ),
    )(doc_blocks, query[0], keys[0], values[0], out_weight, out_grad[0])
    results = pl.pallas_call(
        hand_over,
        out_shape=[jax.ShapeDtypeStruct(a.shape, a.dtype) for a in results],
        in_specs=[vmem] * 5,
        out_specs=[vmem] * 5,
        compiler_params=pltpu.CompilerParams(vmem_limit_bytes=60 << 20),
    )(*results)
    return tuple(a[None] for a in results[:4]) + (results[4],)


def solution(mesh):
    tokens = P("dp", "seq", None)
    return jax.shard_map(
        per_device,
        mesh=mesh,
        in_specs=(tokens, tokens, tokens, P("dp", None), tokens, P("dp", None)),
        out_specs=(tokens, tokens, tokens, tokens, P(("dp", "seq"), None)),
        check_vma=False,
    )
```

```python
import functools

import jax
import jax.numpy as jnp
from jax import lax
from jax.experimental import pallas as pl
from jax.experimental.pallas import tpu as pltpu
from jax.sharding import PartitionSpec as P

HEAD = 256
BLOCK = 128
WINDOW = 1024
SLOTS = 9
ROWS = SLOTS * BLOCK
SPLIT = 1152
MESH = pl.DeviceIdType.MESH
F32 = jnp.float32
BF16 = jnp.bfloat16


def device_at(x, y, z, core):
    return (lax.rem(z, 2) * 4 + x, (lax.div(z, 2) * 4 + y) * 2 + core)


def dot(a, b, ca, cb):
    return lax.dot_general(a, b, (((ca,), (cb,)), ((), ())), preferred_element_type=F32)


def kernel(
    normaliser,
    doc_ref, q_ref, k_ref, v_ref, w_ref, og_ref,
    lo_ref, dq_ref, dk_ref, dv_ref, wg_ref,
    own_st, zbuf, win, qh, og_all, w_all, ga_st, ga, bias, shares, attn_loc, attn_all,
    dq_st, dq_rx, dkv, d0_rx, d4_rx, dy_rx, acc, rel_st, dz_rx,
    wg_st, wy_rx, wsum, wz_rx, wp_st, wp_rx, lp_st, lp_rx, lo_own, lx_st, lx_rx, wx, lt_st, lt_rx, lt_own,
    q_sem, og_s, og_r, ogp_s, ogp_r, w_s, w_r, zk_s, zk_r, yk_s, yk_r, pk_s, pk_r, p0_s, p0_r,
    ga_s, ga_r, at_s, at_r, dqs, dqr, d0s, d0r, d4s, d4r, yd_s, yd_r, zd_s, zd_r,
    wy_s, wy_r, wz_s, wz_r, wp_s, wp_r, lp_s, lp_r, lx_s, lx_r,
    wx_s, wx_r, lt_s, lt_r,
):
    dp = lax.axis_index("dp")
    s = lax.axis_index("seq")
    x, zl = lax.rem(dp, 4), lax.div(dp, 4)
    q, y, zh = lax.rem(s, 2), lax.rem(lax.div(s, 2), 4), lax.div(s, 8)
    z = zh * 2 + zl
    other = 1 - q
    partner = device_at(x, y, z, other)
    scale = HEAD ** (-0.5)
    split = SPLIT

    def mine(i):
        return pl.ds(pl.multiple_of(i * BLOCK, BLOCK), BLOCK)

    def remote(src, dst, ss, rs, dev):
        return pltpu.make_async_remote_copy(
            src_ref=src, dst_ref=dst, send_sem=ss, recv_sem=rs, device_id=dev, device_id_type=MESH
        )

    xs = [lax.rem(x + k, 4) for k in range(4)]
    ys = [lax.rem(y + k, 4) for k in range(4)]

    barrier = pltpu.get_barrier_semaphore()
    count = 0
    for k in range(1, 4):
        pl.semaphore_signal(barrier, 1, device_id=device_at(xs[k], y, z, q), device_id_type=MESH)
        for core in range(2):
            pl.semaphore_signal(
                barrier, 1, device_id=device_at(x, ys[k], z, core), device_id_type=MESH
            )
        count += 3
    pl.semaphore_signal(barrier, 1, device_id=partner, device_id_type=MESH)
    count += 1
    for k in range(1, 8):
        for core in range(2):
            pl.semaphore_signal(
                barrier, 1, device_id=device_at(x, y, lax.rem(z + k, 8), core), device_id_type=MESH
            )
        count += 2

    for half in range(2):
        for m in range(2):
            lo = half * 512 + m * HEAD
            own_st[m, half, :, 0:HEAD] = k_ref[:, lo : lo + HEAD]
            own_st[m, half, :, HEAD : 2 * HEAD] = v_ref[:, lo : lo + HEAD]
    pl.semaphore_wait(barrier, count)

    sends = []

    def go(copy):
        copy.start()
        sends.append(copy)
        return copy

    def up_z(c):
        m, lo, rows = ((0, 0, BLOCK), (1, 0, 64), (1, 64, 64))[c]
        rows = pl.ds(lo, rows)
        return remote(own_st.at[m, :, rows], zbuf.at[m, :, rows], zk_s.at[c], zk_r.at[c],
                      device_at(x, y, lax.rem(z + 2, 8), q))

    def along_y(m, k, half, src, lo=0, rows=BLOCK):
        first = pl.multiple_of((7 - 2 * k + q) * BLOCK + lo, 64)
        return remote(
            src.at[m, half, pl.ds(lo, rows)], win.at[m, pl.ds(first, rows)],
            yk_s.at[m, k - 1, half], yk_r.at[m, k - 1, q], device_at(x, ys[k], z, half),
        )

    def og_send(k):
        return go(remote(og_ref, og_all.at[4 - k, mine(q)], og_s.at[k], og_r.at[4 - k],
                         device_at(xs[k], y, z, q)))

    for c in range(3):
        up_z(c).start()
    og_cp = {1: og_send(1), 3: og_send(3)}
    for m in range(2):
        for k in range(1, 4):
            @pl.when(y + k < 4)
            def _():
                for half in range(2):
                    along_y(m, k, half, own_st).start()

    go(remote(w_ref.at[mine(q)], w_all.at[mine(q)], w_s, w_r.at[q],
              device_at(x, y, lax.rem(z + 7, 8), zl)))
    go(remote(og_ref, og_all.at[0, mine(q)], ogp_s.at[0], ogp_r.at[0], partner))
    for m in range(2):
        go(remote(own_st.at[m, other], win.at[m, mine(7 + q)], pk_s.at[m], pk_r.at[m], partner))
    go(remote(q_ref.at[:, pl.ds(pl.multiple_of(other * 1024, 1024), 1024)], qh.at[mine(q)],
              q_sem.at[0], q_sem.at[1], partner))

    for m in range(2):
        win[m, mine(7 + q), :] = own_st[m, q]
    qh[mine(q), :] = q_ref[:, pl.ds(pl.multiple_of(q * 1024, 1024), 1024)]
    og_all[0, mine(q), :] = og_ref[...]

    chip = zh * 4 + y
    qp = chip * 256 + lax.broadcasted_iota(jnp.int32, (256, 1), 0)
    kp = (chip * 2 - 7) * BLOCK + lax.broadcasted_iota(jnp.int32, (1, ROWS), 1)
    qd = jnp.zeros((256, 1), jnp.int32)
    kd = jnp.zeros((1, ROWS), jnp.int32)
    start = jnp.int32(0)
    for n in range(8):
        qd = qd + (start <= qp).astype(jnp.int32)
        kd = kd + (start <= kp).astype(jnp.int32)
        start = start + doc_ref[0, n] * BLOCK
    allowed = (kp <= qp) & (kp > qp - WINDOW) & (kd == qd)
    bias[...] = jnp.where(allowed, 0.0, -jnp.inf).astype(F32)

    @pl.when(q == zl)
    def _():
        w_all[...] = w_ref[...]

    def relay(c):
        m, lo, rows = ((0, 0, BLOCK), (1, 0, 64), (1, 64, 64))[c]
        up_z(c).wait_recv()
        for k in range(1, 4):
            @pl.when(y + k >= 4)
            def _():
                for half in range(2):
                    along_y(m, k, half, zbuf, lo, rows).start()

        if c == 1:
            return

        @pl.when(q == 1)
        def _():
            remote(zbuf.at[m, 0], win.at[m, pl.ds(0, BLOCK)], p0_s.at[m], p0_r.at[m],
                   partner).start()
            win[m, 0:BLOCK, :] = zbuf[m, 1]

    def og_forward(r):
        og_cp[4 - r].wait_recv()
        go(remote(og_all.at[r, mine(q)], og_all.at[r, mine(q)], ogp_s.at[r], ogp_r.at[r], partner))

    def head_gradient(r):
        remote(og_ref, og_all.at[r, mine(other)], ogp_s.at[r], ogp_r.at[r], partner).wait_recv()
        part = dot(og_all[r], w_all[...], 1, 1).astype(BF16)
        if r == 0:
            ga[x] = part
        else:
            ga_st[r - 1] = part
            go(remote(ga_st.at[r - 1], ga.at[x], ga_s.at[r - 1], ga_r.at[x],
                      device_at(xs[r], y, z, q)))

    def window_wait(m):
        remote(own_st.at[0, 0], win.at[m, mine(7 + other)], pk_s.at[m], pk_r.at[m],
               partner).wait_recv()
        for k in range(1, 4):
            for j in range(2):
                remote(own_st.at[0, 0], win.at[m, mine(7 - 2 * k + j)], yk_s.at[m, 0, 0],
                       yk_r.at[m, k - 1, j], partner).wait_recv()

        @pl.when(q == 0)
        def _():
            remote(zbuf.at[m, 0], win.at[m, pl.ds(0, BLOCK)], p0_s.at[m], p0_r.at[m],
                   partner).wait_recv()

    def lanes(i):
        return pl.ds(pl.multiple_of(i * HEAD, HEAD), HEAD)

    def attn_copy(h):
        r = lax.rem(x - h + 4, 4)
        return remote(attn_loc.at[h], attn_all.at[r], at_s.at[h], at_r.at[r],
                      device_at(jnp.int32(h), y, z, q))

    def forward(m):
        for g in range(2):
            h = m * 2 + g
            scores = dot(qh[:, h * HEAD : h * HEAD + HEAD], win[m, :, 0:HEAD], 1, 1) * scale
            scores = scores + bias[...]
            top = jnp.max(scores, axis=-1, keepdims=True)
            lifted = jnp.exp(scores - top)
            share = lifted * (1.0 / jnp.sum(lifted, axis=-1, keepdims=True))
            shares[g] = share
            attn_loc[h] = dot(share.astype(BF16), win[m, :, HEAD:], 1, 0).astype(BF16)

            @pl.when(x != h)
            def _():
                attn_copy(h).start()

            @pl.when(x == h)
            def _():
                attn_all[0] = attn_loc[h]

    def dy_copy(m, k, j):
        return remote(
            dkv.at[m, pl.ds((7 - 2 * k + j) * BLOCK, BLOCK)], dy_rx.at[m, k - 1, q],
            yd_s.at[m, k - 1, j], yd_r.at[m, k - 1, q], device_at(x, ys[4 - k], z, j))

    def dy_row(m):
        for k in (3, 2, 1):
            @pl.when(y - k >= 0)
            def _():
                for j in range(2):
                    dy_copy(m, k, j).start()

    def backward(m):
        dk = jnp.zeros((ROWS, HEAD), F32)
        dv = jnp.zeros((ROWS, HEAD), F32)
        for g in range(2):
            h = m * 2 + g

            @pl.when(x != h)
            def _():
                remote(ga_st.at[0], ga.at[h], ga_s.at[0], ga_r.at[h], partner).wait_recv()

            share = shares[g]
            gh = ga[h]
            gs = dot(gh, win[m, :, HEAD:], 1, 1)
            centre = jnp.sum(share * gs, axis=-1, keepdims=True)
            ds = (share * (gs - centre) * scale).astype(BF16)
            dq_st[h] = dot(ds, win[m, :, 0:HEAD], 1, 0).astype(BF16)
            dk = dk + dot(ds, qh[:, h * HEAD : h * HEAD + HEAD], 0, 0)
            dv = dv + dot(share.astype(BF16), gh, 0, 0)
        dkv[m, :, 0:HEAD] = dk.astype(BF16)
        dkv[m, :, HEAD:] = dv.astype(BF16)

        for k in (3, 2, 1):
            @pl.when(y - k < 0)
            def _():
                for j in range(2):
                    dy_copy(m, k, j).start()

        if m == 0:
            dy_row(0)

        @pl.when(q == 0)
        def _():
            remote(dkv.at[m, pl.ds(0, BLOCK)], d4_rx.at[m], d4s.at[m], d4r.at[m], partner).start()

        go(remote(dkv.at[m, mine(7 + other)], d0_rx.at[m], d0s.at[m], d0r.at[m], partner))

    def dy_add(m, k):
        for half in range(2):
            remote(own_st.at[0, 0], dy_rx.at[m, k - 1, half], yd_s.at[0, 0, 0],
                   yd_r.at[m, k - 1, half], partner).wait_recv()
        acc[m] += dy_rx[m, k - 1].astype(F32)

    def down_z(m):
        return remote(rel_st.at[m], dz_rx.at[m], zd_s.at[m], zd_r.at[m],
                      device_at(x, y, lax.rem(z + 6, 8), q))

    def relay_sums(m):
        acc[m] = jnp.zeros_like(acc[m])

        @pl.when(q == 1)
        def _():
            remote(own_st.at[0, 0], d4_rx.at[m], d4s.at[m], d4r.at[m], partner).wait_recv()
            acc[m, 0] = d4_rx[m].astype(F32)
            acc[m, 1] = dkv[m, 0:BLOCK, :].astype(F32)

        for k in (3, 2, 1):
            @pl.when(y + k >= 4)
            def _():
                dy_add(m, k)
        rel_st[m] = acc[m].astype(BF16)
        go(down_z(m))

    def own_sums(m):
        remote(own_st.at[0, 0], d0_rx.at[m], d0s.at[m], d0r.at[m], partner).wait_recv()
        acc[m, q] = dkv[m, mine(7 + q), :].astype(F32)
        acc[m, other] = d0_rx[m].astype(F32)
        for k in (3, 2, 1):
            @pl.when(y + k < 4)
            def _():
                dy_add(m, k)

    def own_finish(m):
        down_z(m).wait_recv()
        for half in range(2):
            own = (acc[m, half] + dz_rx[m, half].astype(F32)).astype(BF16)
            lo = half * 512 + m * HEAD
            dk_ref[:, lo : lo + HEAD] = own[:, 0:HEAD]
            dv_ref[:, lo : lo + HEAD] = own[:, HEAD:]

    def weight_wait():
        @pl.when(q != zl)
        def _():
            for j in range(2):
                remote(w_ref.at[pl.ds(0, BLOCK)], w_all.at[pl.ds(j * BLOCK, BLOCK)], w_s,
                       w_r.at[j], partner).wait_recv()

    def query_wait():
        remote(q_ref.at[:, pl.ds(0, 1024)], qh.at[mine(other)], q_sem.at[0], q_sem.at[1],
               partner).wait_recv()

    def attn_wait():
        for r in (1, 3, 2):
            remote(attn_loc.at[0], attn_all.at[r], at_s.at[0], at_r.at[r], partner).wait_recv()

    def wx_copy(k):
        return remote(w_all.at[:, split:], wx.at[x], wx_s.at[k - 1], wx_r.at[x],
                      device_at(xs[k], y, z, q))

    def wx_send():
        wx[x] = w_all[:, split:]
        for k in (1, 3, 2):
            go(wx_copy(k))

    def tail_copy():
        return remote(lt_st, lt_rx, lt_s, lt_r, partner)

    def tail_product():
        for h in range(4):
            @pl.when(x != h)
            def _():
                remote(wx.at[0], wx.at[h], wx_s.at[0], wx_r.at[h], partner).wait_recv()

        lt_st[...] = sum(dot(attn_loc[h, mine(other), :], wx[h], 1, 0) for h in range(4))
        go(tail_copy())
        lt_own[...] = sum(dot(attn_loc[h, mine(q), :], wx[h], 1, 0) for h in range(4))

    def tail_finish():
        tail_copy().wait_recv()
        lo_ref[:, split:] = (lt_own[...] + lt_rx[...]).astype(BF16)

    def lo_pair(r):
        return remote(lp_st.at[r], lp_rx.at[r], lp_s.at[r], lp_r.at[r], partner)

    def lo_product():
        part = dot(attn_all[:, mine(other), :].reshape(512, HEAD), w_all[:, 0:split], 1, 0)
        lp_st[...] = part.astype(BF16).reshape(4, BLOCK, split)
        for r in (1, 3, 2, 0):
            go(lo_pair(r))
        part = dot(attn_all[:, mine(q), :].reshape(512, HEAD), w_all[:, 0:split], 1, 0)
        lo_own[...] = part.reshape(4, BLOCK, split)

    def lo_copy(r):
        return remote(lx_st.at[r - 1], lx_rx.at[r - 1], lx_s.at[r - 1], lx_r.at[r - 1],
                      device_at(xs[r], y, z, q))

    def lo_send(r):
        lo_pair(r).wait_recv()
        lx_st[r - 1] = (lo_own[r] + lp_rx[r].astype(F32)).astype(BF16)
        go(lo_copy(r))

    def lo_finish():
        lo_pair(0).wait_recv()
        out = lo_own[0] + lp_rx[0].astype(F32)
        for r in (1, 3, 2):
            lo_copy(r).wait_recv()
            out = out + lx_rx[r - 1].astype(F32)
        lo_ref[:, 0:split] = out.astype(BF16)

    def wy_copy(k):
        return remote(wg_st.at[ys[k]], wy_rx.at[k - 1], wy_s.at[k - 1], wy_r.at[k - 1],
                      device_at(x, ys[k], z, q))

    def wg_product():
        product = dot(attn_all[...].reshape(1024, HEAD),
                      og_all[...].reshape(1024, og_ref.shape[1]), 0, 0)
        for yy in range(4):
            for zz in range(4):
                wg_st[yy, zz * 16 : zz * 16 + 16, :] = product[
                    (zz * 4 + yy) * 16 : (zz * 4 + yy) * 16 + 16, :
                ].astype(BF16)
        for k in (1, 3, 2):
            go(wy_copy(k))

    def to_z(i):
        return remote(wsum.at[i], wz_rx.at[zh], wz_s.at[i], wz_r.at[zh],
                      device_at(x, y, i * 2 + q, zl))

    def wg_rows():
        total = wg_st[y].astype(F32)
        for k in (1, 3, 2):
            wy_copy(k).wait_recv()
            total = total + wy_rx[k - 1].astype(F32)
        wsum[...] = total.astype(BF16).reshape(4, 16, total.shape[-1])
        for i in range(4):
            here = (i == zh) & (zl == q)

            @pl.when(jnp.logical_not(here))
            def _():
                to_z(i).start()

            @pl.when(here)
            def _():
                wz_rx[zh] = wsum[i]

    def wp_copy():
        return remote(wp_st.at[other], wp_rx, wp_s, wp_r, partner)

    def wg_swap():
        for i in range(4):
            here = (i == zh) & (zl == q)

            @pl.when(jnp.logical_not(here))
            def _():
                remote(wsum.at[0], wz_rx.at[i], wz_s.at[0], wz_r.at[i], partner).wait_recv()

        rows = jnp.sum(wz_rx[...].astype(F32), axis=0)
        wp_st[...] = rows.reshape(2, 8, rows.shape[-1])
        go(wp_copy())

    def wg_finish():
        wp_copy().wait_recv()
        wg_ref[...] = (wp_st[q] + wp_rx[...]) * normaliser

    def dq_copy():
        return remote(dq_st.at[:, mine(other)], dq_rx, dqs, dqr, partner)

    def dq_finish():
        dq_mine = dq_st[:, mine(q), :]
        dq_copy().wait_recv()
        for h in range(4):
            dq_ref[:, lanes(q * 4 + h)] = dq_mine[h]
            dq_ref[:, lanes(other * 4 + h)] = dq_rx[h]

    og_forward(1)
    og_forward(3)
    og_far = 3 - 2 * q
    og_cp[2] = go(remote(og_all.at[og_far, mine(q)], og_all.at[2, mine(q)], og_s.at[2],
                         og_r.at[2], device_at(lax.rem(x + 5 - 2 * q, 4), y, z, q)))
    relay(0)
    weight_wait()
    head_gradient(1)
    head_gradient(3)
    head_gradient(0)
    query_wait()
    relay(1)
    og_forward(2)
    head_gradient(2)
    wx_send()
    window_wait(0)
    forward(0)
    relay(2)
    backward(0)
    window_wait(1)
    forward(1)
    relay_sums(0)
    backward(1)
    go(dq_copy())
    attn_wait()
    wg_product()
    lo_product()
    for r in (1, 3, 2):
        lo_send(r)
    relay_sums(1)
    dy_row(1)
    tail_product()
    dq_finish()
    own_sums(0)
    wg_rows()
    tail_finish()
    wg_swap()
    lo_finish()
    own_sums(1)
    own_finish(0)
    wg_finish()
    own_finish(1)

    for copy in sends:
        copy.wait_send()
    for c in range(3):
        up_z(c).wait_send()
    for m in range(2):
        for k in range(1, 4):
            for half in range(2):
                along_y(m, k, half, own_st).wait_send()
    for m in range(2):
        for k in (3, 2, 1):
            for j in range(2):
                dy_copy(m, k, j).wait_send()
    for h in range(4):
        @pl.when(x != h)
        def _():
            attn_copy(h).wait_send()
    for i in range(4):
        @pl.when(jnp.logical_not((i == zh) & (zl == q)))
        def _():
            to_z(i).wait_send()

    for m in range(2):
        @pl.when(q == 1)
        def _():
            remote(zbuf.at[m, 0], win.at[m, pl.ds(0, BLOCK)], p0_s.at[m], p0_r.at[m],
                   partner).wait_send()

        @pl.when(q == 0)
        def _():
            remote(dkv.at[m, pl.ds(0, BLOCK)], d4_rx.at[m], d4s.at[m], d4r.at[m],
                   partner).wait_send()


def hand_over(*refs):
    for src, dst in zip(refs[:5], refs[5:]):
        dst[...] = src[...]


def per_device(query, keys, values, out_weight, out_grad, doc_blocks):
    width = out_grad.shape[2]
    tokens = lax.axis_size("dp") * lax.axis_size("seq") * BLOCK
    vmem = pl.BlockSpec(memory_space=pltpu.VMEM)
    dma = pltpu.SemaphoreType.DMA
    scratch = [
        ((2, 2, BLOCK, 512), BF16),
        ((2, 2, BLOCK, 512), BF16),
        ((2, ROWS, 512), BF16),
        ((256, 1024), BF16),
        ((4, 256, width), BF16),
        ((HEAD, width), BF16),
        ((3, 256, HEAD), BF16),
        ((4, 256, HEAD), BF16),
        ((256, ROWS), F32),
        ((2, 256, ROWS), F32),
        ((4, 256, HEAD), BF16),
        ((4, 256, HEAD), BF16),
        ((4, 256, HEAD), BF16),
        ((4, BLOCK, HEAD), BF16),
        ((2, ROWS, 512), BF16),
        ((2, BLOCK, 512), BF16),
        ((2, BLOCK, 512), BF16),
        ((2, 3, 2, BLOCK, 512), BF16),
        ((2, 2, BLOCK, 512), F32),
        ((2, 2, BLOCK, 512), BF16),
        ((2, 2, BLOCK, 512), BF16),
        ((4, 64, width), BF16),
        ((3, 64, width), BF16),
        ((4, 16, width), BF16),
        ((4, 16, width), BF16),
        ((2, 8, width), F32),
        ((8, width), F32),
        ((4, BLOCK, SPLIT), BF16),
        ((4, BLOCK, SPLIT), BF16),
        ((4, BLOCK, SPLIT), F32),
        ((3, BLOCK, SPLIT), BF16),
        ((3, BLOCK, SPLIT), BF16),
        ((4, HEAD, width - SPLIT), BF16),
        ((BLOCK, width - SPLIT), F32),
        ((BLOCK, width - SPLIT), F32),
        ((BLOCK, width - SPLIT), F32),
    ]
    semaphores = [
        (2,), (4,), (4,), (4,), (4,), (), (2,), (3,), (3,), (2, 3, 2), (2, 3, 2),
        (2,), (2,), (2,), (2,), (3,), (4,), (4,), (4,), (), (), (2,), (2,), (2,), (2,),
        (2, 3, 2), (2, 3, 2), (2,), (2,),
        (3,), (3,), (4,), (4,), (), (), (4,), (4,), (3,), (3,),
        (3,), (4,), (), (),
    ]
    results = pl.pallas_call(
        functools.partial(kernel, tokens ** (-0.5)),
        out_shape=[
            jax.ShapeDtypeStruct((BLOCK, width), BF16),
            jax.ShapeDtypeStruct((BLOCK, 2048), BF16),
            jax.ShapeDtypeStruct((BLOCK, 1024), BF16),
            jax.ShapeDtypeStruct((BLOCK, 1024), BF16),
            jax.ShapeDtypeStruct((8, width), F32),
        ],
        in_specs=[pl.BlockSpec(memory_space=pltpu.SMEM)] + [vmem] * 5,
        out_specs=[vmem] * 5,
        scratch_shapes=[pltpu.VMEM(*a) for a in scratch]
        + [dma(a) if a else dma for a in semaphores],
        compiler_params=pltpu.CompilerParams(
            collective_id=0, has_side_effects=True, vmem_limit_bytes=60 << 20
        ),
    )(doc_blocks, query[0], keys[0], values[0], out_weight, out_grad[0])
    results = pl.pallas_call(
        hand_over,
        out_shape=[jax.ShapeDtypeStruct(a.shape, a.dtype) for a in results],
        in_specs=[vmem] * 5,
        out_specs=[vmem] * 5,
        compiler_params=pltpu.CompilerParams(vmem_limit_bytes=60 << 20),
    )(*results)
    return tuple(a[None] for a in results[:4]) + (results[4],)


def solution(mesh):
    tokens = P("dp", "seq", None)
    return jax.shard_map(
        per_device,
        mesh=mesh,
        in_specs=(tokens, tokens, tokens, P("dp", None), tokens, P("dp", None)),
        out_specs=(tokens, tokens, tokens, tokens, P(("dp", "seq"), None)),
        check_vma=False,
    )
```

```python
import functools

import jax
import jax.numpy as jnp
from jax import lax
from jax.experimental import pallas as pl
from jax.experimental.pallas import tpu as pltpu
from jax.sharding import PartitionSpec as P

HEAD = 256
BLOCK = 128
WINDOW = 1024
SLOTS = 9
ROWS = SLOTS * BLOCK
SPLIT = 1024
MESH = pl.DeviceIdType.MESH
F32 = jnp.float32
BF16 = jnp.bfloat16


def device_at(x, y, z, core):
    return (lax.rem(z, 2) * 4 + x, (lax.div(z, 2) * 4 + y) * 2 + core)


def dot(a, b, ca, cb):
    return lax.dot_general(a, b, (((ca,), (cb,)), ((), ())), preferred_element_type=F32)


def kernel(
    normaliser,
    doc_ref, q_ref, k_ref, v_ref, w_ref, og_ref,
    lo_ref, dq_ref, dk_ref, dv_ref, wg_ref,
    own_st, zbuf, win, qh, og_all, w_all, ga_st, ga, bias, shares, attn_loc, attn_all,
    dq_st, dq_rx, dkv, d0_rx, d4_rx, dy_rx, acc, rel_st, dz_rx,
    wg_st, wy_rx, wsum, wz_rx, wp_st, wp_rx, lp_st, lp_rx, lo_own, lx_st, lx_rx, wx, lt_st, lt_rx, lt_own,
    q_sem, og_s, og_r, ogp_s, ogp_r, w_s, w_r, zk_s, zk_r, yk_s, yk_r, pk_s, pk_r, p0_s, p0_r,
    ga_s, ga_r, at_s, at_r, dqs, dqr, d0s, d0r, d4s, d4r, yd_s, yd_r, zd_s, zd_r,
    wy_s, wy_r, wz_s, wz_r, wp_s, wp_r, lp_s, lp_r, lx_s, lx_r,
    wx_s, wx_r, lt_s, lt_r,
):
    dp = lax.axis_index("dp")
    s = lax.axis_index("seq")
    x, zl = lax.rem(dp, 4), lax.div(dp, 4)
    q, y, zh = lax.rem(s, 2), lax.rem(lax.div(s, 2), 4), lax.div(s, 8)
    z = zh * 2 + zl
    other = 1 - q
    partner = device_at(x, y, z, other)
    scale = HEAD ** (-0.5)
    split = SPLIT

    def mine(i):
        return pl.ds(pl.multiple_of(i * BLOCK, BLOCK), BLOCK)

    def remote(src, dst, ss, rs, dev):
        return pltpu.make_async_remote_copy(
            src_ref=src, dst_ref=dst, send_sem=ss, recv_sem=rs, device_id=dev, device_id_type=MESH
        )

    xs = [lax.rem(x + k, 4) for k in range(4)]
    ys = [lax.rem(y + k, 4) for k in range(4)]

    barrier = pltpu.get_barrier_semaphore()
    count = 0
    for k in range(1, 4):
        pl.semaphore_signal(barrier, 1, device_id=device_at(xs[k], y, z, q), device_id_type=MESH)
        for core in range(2):
            pl.semaphore_signal(
                barrier, 1, device_id=device_at(x, ys[k], z, core), device_id_type=MESH
            )
        count += 3
    pl.semaphore_signal(barrier, 1, device_id=partner, device_id_type=MESH)
    count += 1
    for k in range(1, 8):
        for core in range(2):
            pl.semaphore_signal(
                barrier, 1, device_id=device_at(x, y, lax.rem(z + k, 8), core), device_id_type=MESH
            )
        count += 2

    for half in range(2):
        for m in range(2):
            lo = half * 512 + m * HEAD
            own_st[m, half, :, 0:HEAD] = k_ref[:, lo : lo + HEAD]
            own_st[m, half, :, HEAD : 2 * HEAD] = v_ref[:, lo : lo + HEAD]
    pl.semaphore_wait(barrier, count)

    sends = []

    def go(copy):
        copy.start()
        sends.append(copy)
        return copy

    def up_z(c):
        m, lo, rows = ((0, 0, BLOCK), (1, 0, 64), (1, 64, 64))[c]
        rows = pl.ds(lo, rows)
        return remote(own_st.at[m, :, rows], zbuf.at[m, :, rows], zk_s.at[c], zk_r.at[c],
                      device_at(x, y, lax.rem(z + 2, 8), q))

    def along_y(m, k, half, src, lo=0, rows=BLOCK):
        first = pl.multiple_of((7 - 2 * k + q) * BLOCK + lo, 64)
        return remote(
            src.at[m, half, pl.ds(lo, rows)], win.at[m, pl.ds(first, rows)],
            yk_s.at[m, k - 1, half], yk_r.at[m, k - 1, q], device_at(x, ys[k], z, half),
        )

    def og_send(k):
        return go(remote(og_ref, og_all.at[4 - k, mine(q)], og_s.at[k], og_r.at[4 - k],
                         device_at(xs[k], y, z, q)))

    for c in range(3):
        up_z(c).start()
    og_cp = {1: og_send(1), 3: og_send(3)}
    for m in range(2):
        for k in range(1, 4):
            @pl.when(y + k < 4)
            def _():
                for half in range(2):
                    along_y(m, k, half, own_st).start()

    go(remote(w_ref.at[mine(q)], w_all.at[mine(q)], w_s, w_r.at[q],
              device_at(x, y, lax.rem(z + 7, 8), zl)))
    go(remote(og_ref, og_all.at[0, mine(q)], ogp_s.at[0], ogp_r.at[0], partner))
    for m in range(2):
        go(remote(own_st.at[m, other], win.at[m, mine(7 + q)], pk_s.at[m], pk_r.at[m], partner))
    go(remote(q_ref.at[:, pl.ds(pl.multiple_of(other * 1024, 1024), 1024)], qh.at[mine(q)],
              q_sem.at[0], q_sem.at[1], partner))

    for m in range(2):
        win[m, mine(7 + q), :] = own_st[m, q]
    qh[mine(q), :] = q_ref[:, pl.ds(pl.multiple_of(q * 1024, 1024), 1024)]
    og_all[0, mine(q), :] = og_ref[...]

    chip = zh * 4 + y
    qp = chip * 256 + lax.broadcasted_iota(jnp.int32, (256, 1), 0)
    kp = (chip * 2 - 7) * BLOCK + lax.broadcasted_iota(jnp.int32, (1, ROWS), 1)
    qd = jnp.zeros((256, 1), jnp.int32)
    kd = jnp.zeros((1, ROWS), jnp.int32)
    start = jnp.int32(0)
    for n in range(8):
        qd = qd + (start <= qp).astype(jnp.int32)
        kd = kd + (start <= kp).astype(jnp.int32)
        start = start + doc_ref[0, n] * BLOCK
    allowed = (kp <= qp) & (kp > qp - WINDOW) & (kd == qd)
    bias[...] = jnp.where(allowed, 0.0, -jnp.inf).astype(F32)

    @pl.when(q == zl)
    def _():
        w_all[...] = w_ref[...]

    def relay(c):
        m, lo, rows = ((0, 0, BLOCK), (1, 0, 64), (1, 64, 64))[c]
        up_z(c).wait_recv()
        for k in range(1, 4):
            @pl.when(y + k >= 4)
            def _():
                for half in range(2):
                    along_y(m, k, half, zbuf, lo, rows).start()

        if c == 1:
            return

        @pl.when(q == 1)
        def _():
            remote(zbuf.at[m, 0], win.at[m, pl.ds(0, BLOCK)], p0_s.at[m], p0_r.at[m],
                   partner).start()
            win[m, 0:BLOCK, :] = zbuf[m, 1]

    def og_forward(r):
        og_cp[4 - r].wait_recv()
        go(remote(og_all.at[r, mine(q)], og_all.at[r, mine(q)], ogp_s.at[r], ogp_r.at[r], partner))

    def head_gradient(r):
        remote(og_ref, og_all.at[r, mine(other)], ogp_s.at[r], ogp_r.at[r], partner).wait_recv()
        part = dot(og_all[r], w_all[...], 1, 1).astype(BF16)
        if r == 0:
            ga[x] = part
        else:
            ga_st[r - 1] = part
            go(remote(ga_st.at[r - 1], ga.at[x], ga_s.at[r - 1], ga_r.at[x],
                      device_at(xs[r], y, z, q)))

    def window_wait(m):
        remote(own_st.at[0, 0], win.at[m, mine(7 + other)], pk_s.at[m], pk_r.at[m],
               partner).wait_recv()
        for k in range(1, 4):
            for j in range(2):
                remote(own_st.at[0, 0], win.at[m, mine(7 - 2 * k + j)], yk_s.at[m, 0, 0],
                       yk_r.at[m, k - 1, j], partner).wait_recv()

        @pl.when(q == 0)
        def _():
            remote(zbuf.at[m, 0], win.at[m, pl.ds(0, BLOCK)], p0_s.at[m], p0_r.at[m],
                   partner).wait_recv()

    def lanes(i):
        return pl.ds(pl.multiple_of(i * HEAD, HEAD), HEAD)

    def attn_copy(h):
        r = lax.rem(x - h + 4, 4)
        return remote(attn_loc.at[h], attn_all.at[r], at_s.at[h], at_r.at[r],
                      device_at(jnp.int32(h), y, z, q))

    def forward(m):
        for g in range(2):
            h = m * 2 + g
            scores = dot(qh[:, h * HEAD : h * HEAD + HEAD], win[m, :, 0:HEAD], 1, 1) * scale
            scores = scores + bias[...]
            top = jnp.max(scores, axis=-1, keepdims=True)
            lifted = jnp.exp(scores - top)
            share = lifted * (1.0 / jnp.sum(lifted, axis=-1, keepdims=True))
            shares[g] = share
            attn_loc[h] = dot(share.astype(BF16), win[m, :, HEAD:], 1, 0).astype(BF16)

            @pl.when(x != h)
            def _():
                attn_copy(h).start()

            @pl.when(x == h)
            def _():
                attn_all[0] = attn_loc[h]

    def dy_copy(m, k, j):
        return remote(
            dkv.at[m, pl.ds((7 - 2 * k + j) * BLOCK, BLOCK)], dy_rx.at[m, k - 1, q],
            yd_s.at[m, k - 1, j], yd_r.at[m, k - 1, q], device_at(x, ys[4 - k], z, j))

    def dy_row(m):
        for k in (3, 2, 1):
            @pl.when(y - k >= 0)
            def _():
                for j in range(2):
                    dy_copy(m, k, j).start()

    def backward(m):
        dk = jnp.zeros((ROWS, HEAD), F32)
        dv = jnp.zeros((ROWS, HEAD), F32)
        for g in range(2):
            h = m * 2 + g

            @pl.when(x != h)
            def _():
                remote(ga_st.at[0], ga.at[h], ga_s.at[0], ga_r.at[h], partner).wait_recv()

            share = shares[g]
            gh = ga[h]
            gs = dot(gh, win[m, :, HEAD:], 1, 1)
            centre = jnp.sum(share * gs, axis=-1, keepdims=True)
            ds = (share * (gs - centre) * scale).astype(BF16)
            dq_st[h] = dot(ds, win[m, :, 0:HEAD], 1, 0).astype(BF16)
            dk = dk + dot(ds, qh[:, h * HEAD : h * HEAD + HEAD], 0, 0)
            dv = dv + dot(share.astype(BF16), gh, 0, 0)
        dkv[m, :, 0:HEAD] = dk.astype(BF16)
        dkv[m, :, HEAD:] = dv.astype(BF16)

        for k in (3, 2, 1):
            @pl.when(y - k < 0)
            def _():
                for j in range(2):
                    dy_copy(m, k, j).start()

        if m == 0:
            dy_row(0)

        @pl.when(q == 0)
        def _():
            remote(dkv.at[m, pl.ds(0, BLOCK)], d4_rx.at[m], d4s.at[m], d4r.at[m], partner).start()

        go(remote(dkv.at[m, mine(7 + other)], d0_rx.at[m], d0s.at[m], d0r.at[m], partner))

    def dy_add(m, k):
        for half in range(2):
            remote(own_st.at[0, 0], dy_rx.at[m, k - 1, half], yd_s.at[0, 0, 0],
                   yd_r.at[m, k - 1, half], partner).wait_recv()
        acc[m] += dy_rx[m, k - 1].astype(F32)

    def down_z(m):
        return remote(rel_st.at[m], dz_rx.at[m], zd_s.at[m], zd_r.at[m],
                      device_at(x, y, lax.rem(z + 6, 8), q))

    def relay_sums(m):
        acc[m] = jnp.zeros_like(acc[m])

        @pl.when(q == 1)
        def _():
            remote(own_st.at[0, 0], d4_rx.at[m], d4s.at[m], d4r.at[m], partner).wait_recv()
            acc[m, 0] = d4_rx[m].astype(F32)
            acc[m, 1] = dkv[m, 0:BLOCK, :].astype(F32)

        for k in (3, 2, 1):
            @pl.when(y + k >= 4)
            def _():
                dy_add(m, k)
        rel_st[m] = acc[m].astype(BF16)
        go(down_z(m))

    def own_sums(m):
        remote(own_st.at[0, 0], d0_rx.at[m], d0s.at[m], d0r.at[m], partner).wait_recv()
        acc[m, q] = dkv[m, mine(7 + q), :].astype(F32)
        acc[m, other] = d0_rx[m].astype(F32)
        for k in (3, 2, 1):
            @pl.when(y + k < 4)
            def _():
                dy_add(m, k)

    def own_finish(m):
        down_z(m).wait_recv()
        for half in range(2):
            own = (acc[m, half] + dz_rx[m, half].astype(F32)).astype(BF16)
            lo = half * 512 + m * HEAD
            dk_ref[:, lo : lo + HEAD] = own[:, 0:HEAD]
            dv_ref[:, lo : lo + HEAD] = own[:, HEAD:]

    def weight_wait():
        @pl.when(q != zl)
        def _():
            for j in range(2):
                remote(w_ref.at[pl.ds(0, BLOCK)], w_all.at[pl.ds(j * BLOCK, BLOCK)], w_s,
                       w_r.at[j], partner).wait_recv()

    def query_wait():
        remote(q_ref.at[:, pl.ds(0, 1024)], qh.at[mine(other)], q_sem.at[0], q_sem.at[1],
               partner).wait_recv()

    def attn_wait():
        for r in (1, 3, 2):
            remote(attn_loc.at[0], attn_all.at[r], at_s.at[0], at_r.at[r], partner).wait_recv()

    def wx_copy(k):
        return remote(w_all.at[:, split:], wx.at[x], wx_s.at[k - 1], wx_r.at[x],
                      device_at(xs[k], y, z, q))

    def wx_send():
        wx[x] = w_all[:, split:]
        for k in (1, 3, 2):
            go(wx_copy(k))

    def tail_copy():
        return remote(lt_st, lt_rx, lt_s, lt_r, partner)

    def tail_product():
        for h in range(4):
            @pl.when(x != h)
            def _():
                remote(wx.at[0], wx.at[h], wx_s.at[0], wx_r.at[h], partner).wait_recv()

        lt_st[...] = sum(dot(attn_loc[h, mine(other), :], wx[h], 1, 0) for h in range(4))
        go(tail_copy())
        lt_own[...] = sum(dot(attn_loc[h, mine(q), :], wx[h], 1, 0) for h in range(4))

    def tail_finish():
        tail_copy().wait_recv()
        lo_ref[:, split:] = (lt_own[...] + lt_rx[...]).astype(BF16)

    def lo_pair(r):
        return remote(lp_st.at[r], lp_rx.at[r], lp_s.at[r], lp_r.at[r], partner)

    def lo_product():
        part = dot(attn_all[:, mine(other), :].reshape(512, HEAD), w_all[:, 0:split], 1, 0)
        lp_st[...] = part.astype(BF16).reshape(4, BLOCK, split)
        for r in (1, 3, 2, 0):
            go(lo_pair(r))
        part = dot(attn_all[:, mine(q), :].reshape(512, HEAD), w_all[:, 0:split], 1, 0)
        lo_own[...] = part.reshape(4, BLOCK, split)

    def lo_copy(r):
        return remote(lx_st.at[r - 1], lx_rx.at[r - 1], lx_s.at[r - 1], lx_r.at[r - 1],
                      device_at(xs[r], y, z, q))

    def lo_send(r):
        lo_pair(r).wait_recv()
        lx_st[r - 1] = (lo_own[r] + lp_rx[r].astype(F32)).astype(BF16)
        go(lo_copy(r))

    def lo_finish():
        lo_pair(0).wait_recv()
        out = lo_own[0] + lp_rx[0].astype(F32)
        for r in (1, 3, 2):
            lo_copy(r).wait_recv()
            out = out + lx_rx[r - 1].astype(F32)
        lo_ref[:, 0:split] = out.astype(BF16)

    def wy_copy(k):
        return remote(wg_st.at[ys[k]], wy_rx.at[k - 1], wy_s.at[k - 1], wy_r.at[k - 1],
                      device_at(x, ys[k], z, q))

    def wg_product():
        product = dot(attn_all[...].reshape(1024, HEAD),
                      og_all[...].reshape(1024, og_ref.shape[1]), 0, 0)
        for yy in range(4):
            for zz in range(4):
                wg_st[yy, zz * 16 : zz * 16 + 16, :] = product[
                    (zz * 4 + yy) * 16 : (zz * 4 + yy) * 16 + 16, :
                ].astype(BF16)
        for k in (1, 3, 2):
            go(wy_copy(k))

    def to_z(i):
        return remote(wsum.at[i], wz_rx.at[zh], wz_s.at[i], wz_r.at[zh],
                      device_at(x, y, i * 2 + q, zl))

    def wg_rows():
        total = wg_st[y].astype(F32)
        for k in (1, 3, 2):
            wy_copy(k).wait_recv()
            total = total + wy_rx[k - 1].astype(F32)
        wsum[...] = total.astype(BF16).reshape(4, 16, total.shape[-1])
        for i in range(4):
            here = (i == zh) & (zl == q)

            @pl.when(jnp.logical_not(here))
            def _():
                to_z(i).start()

            @pl.when(here)
            def _():
                wz_rx[zh] = wsum[i]

    def wp_copy():
        return remote(wp_st.at[other], wp_rx, wp_s, wp_r, partner)

    def wg_swap():
        for i in range(4):
            here = (i == zh) & (zl == q)

            @pl.when(jnp.logical_not(here))
            def _():
                remote(wsum.at[0], wz_rx.at[i], wz_s.at[0], wz_r.at[i], partner).wait_recv()

        rows = jnp.sum(wz_rx[...].astype(F32), axis=0)
        wp_st[...] = rows.reshape(2, 8, rows.shape[-1])
        go(wp_copy())

    def wg_finish():
        wp_copy().wait_recv()
        wg_ref[...] = (wp_st[q] + wp_rx[...]) * normaliser

    def dq_copy():
        return remote(dq_st.at[:, mine(other)], dq_rx, dqs, dqr, partner)

    def dq_finish():
        dq_mine = dq_st[:, mine(q), :]
        dq_copy().wait_recv()
        for h in range(4):
            dq_ref[:, lanes(q * 4 + h)] = dq_mine[h]
            dq_ref[:, lanes(other * 4 + h)] = dq_rx[h]

    og_forward(1)
    og_forward(3)
    og_far = 3 - 2 * q
    og_cp[2] = go(remote(og_all.at[og_far, mine(q)], og_all.at[2, mine(q)], og_s.at[2],
                         og_r.at[2], device_at(lax.rem(x + 5 - 2 * q, 4), y, z, q)))
    relay(0)
    weight_wait()
    head_gradient(1)
    head_gradient(3)
    head_gradient(0)
    query_wait()
    relay(1)
    og_forward(2)
    head_gradient(2)
    wx_send()
    window_wait(0)
    forward(0)
    relay(2)
    backward(0)
    window_wait(1)
    forward(1)
    relay_sums(0)
    backward(1)
    go(dq_copy())
    attn_wait()
    wg_product()
    lo_product()
    for r in (1, 3, 2):
        lo_send(r)
    relay_sums(1)
    dy_row(1)
    tail_product()
    dq_finish()
    own_sums(0)
    wg_rows()
    tail_finish()
    wg_swap()
    lo_finish()
    own_sums(1)
    own_finish(0)
    wg_finish()
    own_finish(1)

    for copy in sends:
        copy.wait_send()
    for c in range(3):
        up_z(c).wait_send()
    for m in range(2):
        for k in range(1, 4):
            for half in range(2):
                along_y(m, k, half, own_st).wait_send()
    for m in range(2):
        for k in (3, 2, 1):
            for j in range(2):
                dy_copy(m, k, j).wait_send()
    for h in range(4):
        @pl.when(x != h)
        def _():
            attn_copy(h).wait_send()
    for i in range(4):
        @pl.when(jnp.logical_not((i == zh) & (zl == q)))
        def _():
            to_z(i).wait_send()

    for m in range(2):
        @pl.when(q == 1)
        def _():
            remote(zbuf.at[m, 0], win.at[m, pl.ds(0, BLOCK)], p0_s.at[m], p0_r.at[m],
                   partner).wait_send()

        @pl.when(q == 0)
        def _():
            remote(dkv.at[m, pl.ds(0, BLOCK)], d4_rx.at[m], d4s.at[m], d4r.at[m],
                   partner).wait_send()


def hand_over(*refs):
    for src, dst in zip(refs[:5], refs[5:]):
        dst[...] = src[...]


def per_device(query, keys, values, out_weight, out_grad, doc_blocks):
    width = out_grad.shape[2]
    tokens = lax.axis_size("dp") * lax.axis_size("seq") * BLOCK
    vmem = pl.BlockSpec(memory_space=pltpu.VMEM)
    dma = pltpu.SemaphoreType.DMA
    scratch = [
        ((2, 2, BLOCK, 512), BF16),
        ((2, 2, BLOCK, 512), BF16),
        ((2, ROWS, 512), BF16),
        ((256, 1024), BF16),
        ((4, 256, width), BF16),
        ((HEAD, width), BF16),
        ((3, 256, HEAD), BF16),
        ((4, 256, HEAD), BF16),
        ((256, ROWS), F32),
        ((2, 256, ROWS), F32),
        ((4, 256, HEAD), BF16),
        ((4, 256, HEAD), BF16),
        ((4, 256, HEAD), BF16),
        ((4, BLOCK, HEAD), BF16),
        ((2, ROWS, 512), BF16),
        ((2, BLOCK, 512), BF16),
        ((2, BLOCK, 512), BF16),
        ((2, 3, 2, BLOCK, 512), BF16),
        ((2, 2, BLOCK, 512), F32),
        ((2, 2, BLOCK, 512), BF16),
        ((2, 2, BLOCK, 512), BF16),
        ((4, 64, width), BF16),
        ((3, 64, width), BF16),
        ((4, 16, width), BF16),
        ((4, 16, width), BF16),
        ((2, 8, width), F32),
        ((8, width), F32),
        ((4, BLOCK, SPLIT), BF16),
        ((4, BLOCK, SPLIT), BF16),
        ((4, BLOCK, SPLIT), F32),
        ((3, BLOCK, SPLIT), BF16),
        ((3, BLOCK, SPLIT), BF16),
        ((4, HEAD, width - SPLIT), BF16),
        ((BLOCK, width - SPLIT), F32),
        ((BLOCK, width - SPLIT), F32),
        ((BLOCK, width - SPLIT), F32),
    ]
    semaphores = [
        (2,), (4,), (4,), (4,), (4,), (), (2,), (3,), (3,), (2, 3, 2), (2, 3, 2),
        (2,), (2,), (2,), (2,), (3,), (4,), (4,), (4,), (), (), (2,), (2,), (2,), (2,),
        (2, 3, 2), (2, 3, 2), (2,), (2,),
        (3,), (3,), (4,), (4,), (), (), (4,), (4,), (3,), (3,),
        (3,), (4,), (), (),
    ]
    results = pl.pallas_call(
        functools.partial(kernel, tokens ** (-0.5)),
        out_shape=[
            jax.ShapeDtypeStruct((BLOCK, width), BF16),
            jax.ShapeDtypeStruct((BLOCK, 2048), BF16),
            jax.ShapeDtypeStruct((BLOCK, 1024), BF16),
            jax.ShapeDtypeStruct((BLOCK, 1024), BF16),
            jax.ShapeDtypeStruct((8, width), F32),
        ],
        in_specs=[pl.BlockSpec(memory_space=pltpu.SMEM)] + [vmem] * 5,
        out_specs=[vmem] * 5,
        scratch_shapes=[pltpu.VMEM(*a) for a in scratch]
        + [dma(a) if a else dma for a in semaphores],
        compiler_params=pltpu.CompilerParams(
            collective_id=0, has_side_effects=True, vmem_limit_bytes=60 << 20
        ),
    )(doc_blocks, query[0], keys[0], values[0], out_weight, out_grad[0])
    results = pl.pallas_call(
        hand_over,
        out_shape=[jax.ShapeDtypeStruct(a.shape, a.dtype) for a in results],
        in_specs=[vmem] * 5,
        out_specs=[vmem] * 5,
        compiler_params=pltpu.CompilerParams(vmem_limit_bytes=60 << 20),
    )(*results)
    return tuple(a[None] for a in results[:4]) + (results[4],)


def solution(mesh):
    tokens = P("dp", "seq", None)
    return jax.shard_map(
        per_device,
        mesh=mesh,
        in_specs=(tokens, tokens, tokens, P("dp", None), tokens, P("dp", None)),
        out_specs=(tokens, tokens, tokens, tokens, P(("dp", "seq"), None)),
        check_vma=False,
    )
```
